128 devices in a mesh: head: 4 (over x_lo, core), outer: 2 (over x_hi), inner: 16 (over z, y).
Axes of the slice: x: 4 (x_hi: 2, x_lo: 2; x = x_hi * 2 + x_lo), y: 4, z: 4, core: 2. Of those that a mesh axis runs over, the one named last changes fastest.
Arguments:
- queries: bfloat16 [8192, 8192], P(('outer', 'inner'), 'head'), may hold values from -128 to 128
- keys: bfloat16 [8192, 1024], P(('outer', 'inner'), 'head'), may hold values from -6 to 6
- values: bfloat16 [8192, 1024], P(('outer', 'inner'), 'head'), may hold values from -6 to 6
- segment_ids: int32 [8192], P(('outer', 'inner')), may hold values from 0 to 7, never falling along the last dimension, each value on 1 to 6144 neighbouring positions
- value_weight: float32 [8192], P('head'), may hold values from -0.3 to 0.3
- targets: float32 [8192], P(('outer', 'inner')), may hold values from -6 to 6
- upstream: bfloat16 [8192, 8192], P(('outer', 'inner'), 'head'), may hold values from -6 to 6
Outputs:
- query_grad: bfloat16 [8192, 8192], P(('outer', 'inner'), 'head')
- key_grad: bfloat16 [8192, 1024], P(('outer', 'inner'), 'head')
- value_grad: bfloat16 [8192, 1024], P(('outer', 'inner'), 'head')
- value_error: float32 [8192], P(('outer', 'inner'))
- readout_grad: float32 [8192], P('head')
The draws below stay inside these ranges and needn't reach their ends.
Inputs may be any that keep to these rules, and one draw needn't show every extreme that they name: `segment_ids`: segment numbers never fall along the tokens; a segment holds at most 6144 tokens, and one holds exactly that many.
All inputs are finite; a program needn't handle non-finite values.
Results may differ from the reference program's by a relative error of at most 0.027.
Values may be sent and summed in bfloat16 or wider, within the bound.
No kernel may reach another device: no remote copies, remote signals or barrier semaphores. Data moves between devices by JAX's collectives and lax.ppermute only.
A program may use at most 448 MiB of HBM per device.

```python
import math
import jax
import jax.numpy as jnp
import numpy as np
from jax import lax

HD = 128
QH = 64
KVH = 8
GROUP = 8
LENGTH = 8192
SEG_COUNT = 8


def shared_keys(key):
    return jax.random.truncated_normal(key, -6.0, 6.0, (LENGTH, KVH, HD), jnp.float32)


def draw_keys(key, part):
    base_keys = shared_keys(key)
    return base_keys.reshape(LENGTH, KVH * HD).astype(jnp.bfloat16)


def draw_queries(key, part):
    key = jax.random.fold_in(key, 9)
    fresh = jax.random.truncated_normal(key, -6.0, 6.0, (LENGTH, KVH, GROUP, HD), jnp.float32)
    return fresh.reshape(LENGTH, QH * HD).astype(jnp.bfloat16)


def level_of(rng, dims, cuts, least, largest):
    level = 1.0
    for position, blocks in cuts:
        draws = jax.random.uniform(jax.random.fold_in(jax.random.fold_in(rng, 6), position), (blocks,), jnp.float32, least / len(cuts), largest / len(cuts))
        level = level * jnp.repeat(jnp.exp(draws), dims[position] // blocks).reshape((-1,) + (1,) * (len(dims) - 1 - position))
    return level


def profile(number_of, total, reach, lean):
    weights = [(1 << 20) // math.isqrt(standing ** lean) + 1 for standing in range(2, number_of + 1)]
    surplus, given = total - reach - (number_of - 1), [1] * (number_of - 1)
    while surplus > 0:
        candidates = [i for i in range(number_of - 1) if given[i] < reach]
        pool, budget = sum([weights[i] for i in candidates]), surplus
        for i in candidates:
            extra = min(reach - given[i], max(1, budget * weights[i] // pool), surplus)
            given[i] = given[i] + extra
            surplus = surplus - extra
    return np.array([reach] + given)


def ragged_sizes(stream_key, number_of, total, bound, lean):
    if number_of == 2:
        one = jax.random.randint(stream_key, (), max(1, total - bound), min(bound, total - 1) + 1)
        return jnp.stack([one, total - one])
    lengths = jnp.asarray(profile(number_of, total, bound, lean), jnp.int32)
    pairs = (number_of - 1) // 2
    giver, taker = lengths[1:1 + 2 * pairs:2], lengths[2:2 + 2 * pairs:2]
    slack = jnp.minimum(giver - 1, bound - taker)
    shifted = jax.random.randint(jax.random.fold_in(stream_key, 1), (pairs,), 0, 1 << 20) % (slack + 1)
    lengths = lengths.at[1:1 + 2 * pairs:2].set(giver - shifted).at[2:2 + 2 * pairs:2].set(taker + shifted)
    return lengths[jax.random.permutation(jax.random.fold_in(stream_key, 2), number_of)]


def noise(key, shape, scale, bound, pieces=(), kind=jnp.bfloat16):
    entries = jax.random.normal(key, shape, jnp.float32) * scale
    if len(pieces) > 0:
        entries = level_of(key, shape, pieces, -0.22, 0.18) * entries
    return jnp.clip(entries, min=-bound, max=bound).astype(kind)


def setup_inputs(seed: int = 0) -> dict:
    arg_keys = jax.random.split(jax.random.key(seed), 8)
    queries = draw_queries(jax.random.fold_in(arg_keys[7], 71), 0)
    keys = draw_keys(jax.random.fold_in(arg_keys[7], 71), 0)
    values = noise(arg_keys[2], (LENGTH, KVH * HD), 1.0, 6.0, ((0, 32), (1, 4)))
    segment_ids = jnp.searchsorted(jnp.cumsum(ragged_sizes(arg_keys[3], SEG_COUNT, LENGTH, 3 * LENGTH // 4, 0)), jnp.arange(LENGTH), side="right").astype(jnp.int32)
    value_weight = noise(arg_keys[4], (QH * HD,), 0.05, 0.3, ((0, 4),), jnp.float32)
    targets = noise(arg_keys[5], (LENGTH,), 1.0, 6.0, ((0, 32),), jnp.float32)
    upstream = noise(arg_keys[6], (LENGTH, QH * HD), 1.0, 6.0, ((0, 32), (1, 4)))
    return dict(queries=queries, keys=keys, values=values, segment_ids=segment_ids, value_weight=value_weight, targets=targets, upstream=upstream)


def allowed_pairs(query_pos, query_seg, key_pos, key_seg):
    return (key_pos[None, :] <= query_pos[:, None]) & (key_seg[None, :] == query_seg[:, None])


def reference(queries, keys, values, segment_ids, value_weight, targets, upstream):
    seq_len = queries.shape[0]
    score_scale = HD ** -0.5
    positions = jnp.arange(seq_len, dtype=jnp.int32)
    query_heads = queries.reshape(seq_len, KVH, GROUP, HD).astype(jnp.float32)
    key_heads = keys.reshape(seq_len, KVH, HD).astype(jnp.float32)
    value_heads = values.reshape(seq_len, KVH, HD).astype(jnp.float32)
    q_block = min(seq_len, 512)
    n_blocks = seq_len // q_block

    def block_logits(step_index):
        offset = (step_index * q_block).astype(jnp.int32)
        query_blk = lax.dynamic_slice_in_dim(query_heads, offset, q_block, 0)
        query_pos = offset + jnp.arange(q_block, dtype=jnp.int32)
        query_seg = lax.dynamic_slice_in_dim(segment_ids, offset, q_block, 0)
        allowed = allowed_pairs(query_pos, query_seg, positions, segment_ids)
        logits = jnp.einsum('qhgd,khd->hgqk', query_blk, key_heads) * score_scale
        return query_blk, allowed, logits

    def forward_block(step_index):
        query_blk, allowed, logits = block_logits(step_index)
        masked = jnp.where(allowed, logits, -1e30)
        row_max = jnp.max(masked, -1)
        weights = jnp.where(allowed, jnp.exp(logits - row_max[..., None]), 0.0)
        totals = jnp.sum(weights, -1)
        weights_low = lax.optimization_barrier(weights.astype(jnp.bfloat16)).astype(jnp.float32)
        mixed = jnp.einsum('hgqk,khd->qhgd', weights_low, value_heads)
        mixed = mixed / totals.transpose(2, 0, 1)[..., None]
        return mixed.astype(jnp.bfloat16), row_max + jnp.log(totals)

    attn_blocks, lse_blocks = lax.map(forward_block, jnp.arange(n_blocks, dtype=jnp.int32))
    attn_out = attn_blocks.reshape(seq_len, KVH, GROUP, HD)
    lse = lse_blocks.transpose(1, 2, 0, 3).reshape(KVH, GROUP, seq_len)
    attn_flat = attn_out.reshape(seq_len, QH * HD).astype(jnp.float32)
    critic = jnp.sum(attn_flat * value_weight[None, :], -1)
    value_error = critic - targets
    readout_grad = jnp.sum(value_error[:, None] * attn_flat, 0)
    dout = (value_error[:, None] * value_weight[None, :] + upstream.astype(jnp.float32)).astype(jnp.bfloat16)
    dout_heads = dout.reshape(seq_len, KVH, GROUP, HD).astype(jnp.float32)
    row_delta = jnp.sum(dout_heads * attn_out.astype(jnp.float32), -1).transpose(1, 2, 0)

    def backward_block(carried, step_index):
        grad_keys, grad_values = carried
        query_blk, allowed, logits = block_logits(step_index)
        offset = (step_index * q_block).astype(jnp.int32)
        lse_blk = lax.dynamic_slice_in_dim(lse, offset, q_block, 2)
        delta_blk = lax.dynamic_slice_in_dim(row_delta, offset, q_block, 2)
        dout_blk = lax.dynamic_slice_in_dim(dout_heads, offset, q_block, 0)
        attn_prob = jnp.where(allowed, jnp.exp(logits - lse_blk[..., None]), 0.0)
        prob_low = lax.optimization_barrier(attn_prob.astype(jnp.bfloat16)).astype(jnp.float32)
        dprob = jnp.einsum('qhgd,khd->hgqk', dout_blk, value_heads)
        dlogit = lax.optimization_barrier((attn_prob * (dprob - delta_blk[..., None])).astype(jnp.bfloat16)).astype(jnp.float32)
        grad_query = jnp.einsum('hgqk,khd->qhgd', dlogit, key_heads) * score_scale
        grad_keys = grad_keys + jnp.einsum('hgqk,qhgd->khd', dlogit, query_blk) * score_scale
        grad_values = grad_values + jnp.einsum('hgqk,qhgd->khd', prob_low, dout_blk)
        return (grad_keys, grad_values), grad_query.astype(jnp.bfloat16)

    zeros_kv = jnp.zeros((seq_len, KVH, HD), jnp.float32)
    (grad_keys, grad_values), grad_blocks = lax.scan(backward_block, (zeros_kv, zeros_kv), jnp.arange(n_blocks, dtype=jnp.int32))
    query_grad = grad_blocks.reshape(seq_len, QH * HD)
    key_grad = grad_keys.reshape(seq_len, KVH * HD).astype(jnp.bfloat16)
    value_grad = grad_values.reshape(seq_len, KVH * HD).astype(jnp.bfloat16)
    return (query_grad, key_grad, value_grad, value_error, readout_grad)
```

```python
import functools
import math

import jax
import jax.numpy as jnp
from jax import lax
from jax.experimental import pallas as pl
from jax.experimental.pallas import tpu as pltpu
from jax.sharding import PartitionSpec as P

HD = 128
BLK = 256
NB = 32
HPD = 4
WIDTH = HPD * HD
PAD = 16
SCALE = HD ** (-0.5)
SCALE2 = SCALE * math.log2(math.e)
NEG = -1e30
CTX = ("outer", "inner")
NT = (((1,), (1,)), ((), ()))
F32 = jnp.float32
BF16 = jnp.bfloat16
VMEM_LIMIT = 52 * 1024 * 1024


def dot(a, b):
    return jnp.dot(a, b, preferred_element_type=F32)


def dot_nt(a, b):
    return lax.dot_general(a, b, NT, preferred_element_type=F32)


def rows(b):
    return pl.ds(pl.multiple_of(b * BLK, BLK), BLK)


def block_of(scal, o, dz, dy):
    z = (scal[12] + dz) & 3
    y = (scal[13] + dy) & 3
    return 16 * o + 4 * z + y


def place_keys(scal, kp, put):
    for dy in range(4):
        for dz in range(4):
            for o in range(2):
                put(block_of(scal, o, dz, dy), kp[dy][dz, o, :BLK, :])


def place_values(scal, vp, put):
    for dz in range(4):
        for dy in range(4):
            for o in range(2):
                put(block_of(scal, o, dz, dy), vp[dz][dy, o])


def start_of(scal, pos):
    lo = jnp.zeros_like(pos)
    for v in range(1, 8):
        lo = jnp.maximum(lo, jnp.where(pos >= scal[v], scal[v], 0))
    return lo


def allowed_of(scal, base, kb):
    query_pos = base + lax.broadcasted_iota(jnp.int32, (1, BLK), 1)
    lo = start_of(scal, query_pos)
    key_pos = kb * BLK + lax.broadcasted_iota(jnp.int32, (BLK, BLK), 0)
    return (key_pos <= query_pos) & (key_pos >= lo)


def sweep(scal, base, body):
    diag = base // BLK
    first = start_of(scal, base) // BLK
    full = (start_of(scal, base + BLK - 1) + BLK - 1) // BLK
    full = jnp.minimum(full, diag)

    def masked(t, c):
        kb = jnp.where(t == 0, diag, first + t - 1)
        body(kb, True)
        return c

    def plain(kb, c):
        body(kb, False)
        return c

    lax.fori_loop(0, full - first + 1, masked, 0)
    lax.fori_loop(full, diag, plain, 0)


def forward_kernel(
    scal, q0, q1, q2, q3, k0, k1, k2, k3, v0, v1, v2, v3, w_ref,
    out_ref, lse_ref, critic_ref,
    q_all, k_all, vt_all, acc, top, tot,
):
    for p, q in enumerate((q0, q1, q2, q3)):
        q_all[p] = q[...]

    def put_k(b, blk):
        k_all[rows(b), :] = blk

    def put_v(b, blk):
        vt_all[b] = blk.T

    place_keys(scal, (k0, k1, k2, k3), put_k)
    place_values(scal, (v0, v1, v2, v3), put_v)

    def piece(p, c):
        base = scal[8 + p]
        top[...] = jnp.full_like(top, NEG)
        tot[...] = jnp.zeros_like(tot)
        acc[...] = jnp.zeros_like(acc)

        def body(kb, masked):
            k_blk = k_all[rows(kb), :]
            vt_blk = vt_all[kb]
            if masked:
                allowed = allowed_of(scal, base, kb)
            for h in range(HPD):
                s = dot_nt(k_blk, q_all[p, :, h * HD:(h + 1) * HD])
                if masked:
                    s = jnp.where(allowed, s, NEG)
                old = top[h]
                new = jnp.maximum(old, jnp.max(s, 0, keepdims=True))
                prob = jnp.exp2(s * SCALE2 - new * SCALE2)
                fade = jnp.exp2((old - new) * SCALE2)
                top[h] = new
                tot[h] = tot[h] * fade + jnp.sum(prob, 0, keepdims=True)
                acc[h] = acc[h] * fade + dot(vt_blk, prob.astype(BF16))

        sweep(scal, base, body)
        critic = jnp.zeros((1, BLK), F32)
        for h in range(HPD):
            total = tot[h]
            out = (acc[h] / total).astype(BF16)
            out_ref[p, h] = out
            lse_ref[p, h] = top[h] * SCALE2 + jnp.log2(total)
            w = w_ref[h * HD:(h + 1) * HD, :]
            critic += jnp.sum(out.astype(F32) * jnp.concatenate([w, w], 1), 0, keepdims=True)
        critic_ref[p] = critic
        return c

    lax.fori_loop(0, 4, piece, 0)


def backward_kernel(
    scal, q0, q1, q2, q3, u0, u1, u2, u3, k0, k1, k2, k3, v0, v1, v2, v3,
    w_ref, out_ref, lse_ref, err_ref,
    dq_ref, dk0, dk1, dk2, dk3, dv0, dv1, dv2, dv3, readout_ref,
    q_all, k_all, kt_all, v_all, do_all, dot_all, delta_all, dk_all, dv_all, dqt,
):
    for p, q in enumerate((q0, q1, q2, q3)):
        q_all[p] = q[...]

    def put_k(b, blk):
        k_all[rows(b), :] = blk
        kt_all[b] = blk.T

    def put_v(b, blk):
        v_all[rows(b), :] = blk

    place_keys(scal, (k0, k1, k2, k3), put_k)
    place_values(scal, (v0, v1, v2, v3), put_v)
    dk_all[...] = jnp.zeros_like(dk_all)
    dv_all[...] = jnp.zeros_like(dv_all)
    for h in range(HPD):
        cols = slice(h * HD, (h + 1) * HD)
        w = w_ref[cols, :]
        w = jnp.concatenate([w, w], 1)
        readout = jnp.zeros((HD, BLK), F32)
        for p, u in enumerate((u0, u1, u2, u3)):
            err = err_ref[p]
            out = out_ref[p, h].astype(F32)
            dout = (err * w + u[:, cols].T.astype(F32)).astype(BF16)
            dot_all[p, h] = dout
            do_all[p, h] = dout.T
            delta_all[p, h] = jnp.sum(dout.astype(F32) * out, 0, keepdims=True)
            readout += err * out
        readout_ref[cols, :] = jnp.sum(readout, 1, keepdims=True)

    def piece(p, c):
        base = scal[8 + p]
        dqt[...] = jnp.zeros_like(dqt)

        def body(kb, masked):
            k_blk = k_all[rows(kb), :]
            v_blk = v_all[rows(kb), :]
            kt_blk = kt_all[kb]
            if masked:
                allowed = allowed_of(scal, base, kb)
            dk = jnp.zeros((BLK, HD), F32)
            dv = jnp.zeros((BLK, HD), F32)
            for h in range(HPD):
                q = q_all[p, :, h * HD:(h + 1) * HD]
                prob = jnp.exp2(dot_nt(k_blk, q) * SCALE2 - lse_ref[p, h])
                if masked:
                    prob = jnp.where(allowed, prob, 0.0)
                dprob = dot(v_blk, dot_all[p, h])
                dlogit = (prob * (dprob - delta_all[p, h])).astype(BF16)
                dv += dot(prob.astype(BF16), do_all[p, h])
                dk += dot(dlogit, q)
                dqt[h] += dot(kt_blk, dlogit)
            dk_all[rows(kb), :] += dk
            dv_all[rows(kb), :] += dv

        sweep(scal, base, body)
        for h in range(HPD):
            dq_ref[p, :, h * HD:(h + 1) * HD] = (dqt[h] * SCALE).T.astype(BF16)
        return c

    lax.fori_loop(0, 4, piece, 0)

    for dy, dk in enumerate((dk0, dk1, dk2, dk3)):
        for dz in range(4):
            for o in range(2):
                b = block_of(scal, o, dz, dy)
                dk[dz, o] = (dk_all[rows(b), :] * SCALE).astype(BF16)
    for dz, dv in enumerate((dv0, dv1, dv2, dv3)):
        for dy in range(4):
            for o in range(2):
                b = block_of(scal, o, dz, dy)
                dv[dy, o] = dv_all[rows(b), :].astype(BF16)


SMEM_SPEC = pl.BlockSpec(memory_space=pltpu.SMEM)
VMEM_SPEC = pl.BlockSpec(memory_space=pltpu.VMEM)


def forward(scal, qs, kp, vp, w):
    return pl.pallas_call(
        forward_kernel,
        out_shape=(
            jax.ShapeDtypeStruct((4, HPD, HD, BLK), BF16),
            jax.ShapeDtypeStruct((4, HPD, 1, BLK), F32),
            jax.ShapeDtypeStruct((4, 1, BLK), F32),
        ),
        in_specs=[SMEM_SPEC] + [VMEM_SPEC] * 13,
        out_specs=(VMEM_SPEC,) * 3,
        scratch_shapes=[
            pltpu.VMEM((4, BLK, WIDTH), BF16),
            pltpu.VMEM((NB * BLK, HD), BF16),
            pltpu.VMEM((NB, HD, BLK), BF16),
            pltpu.VMEM((HPD, HD, BLK), F32),
            pltpu.VMEM((HPD, 1, BLK), F32),
            pltpu.VMEM((HPD, 1, BLK), F32),
        ],
        compiler_params=pltpu.CompilerParams(vmem_limit_bytes=VMEM_LIMIT),
        cost_estimate=pl.CostEstimate(flops=9 * 10**9, bytes_accessed=8 << 20, transcendentals=10**7),
        name="attention_forward",
    )(scal, *qs, *kp, *vp, w)


def backward(scal, qs, us, kp, vp, w, out, lse, err):
    piece = jax.ShapeDtypeStruct((4, 2, BLK, HD), BF16)
    return pl.pallas_call(
        backward_kernel,
        out_shape=(
            jax.ShapeDtypeStruct((4, BLK, WIDTH), BF16),
            *([piece] * 8),
            jax.ShapeDtypeStruct((WIDTH, 1), F32),
        ),
        in_specs=[SMEM_SPEC] + [VMEM_SPEC] * 20,
        out_specs=(VMEM_SPEC,) * 10,
        scratch_shapes=[
            pltpu.VMEM((4, BLK, WIDTH), BF16),
            pltpu.VMEM((NB * BLK, HD), BF16),
            pltpu.VMEM((NB, HD, BLK), BF16),
            pltpu.VMEM((NB * BLK, HD), BF16),
            pltpu.VMEM((4, HPD, BLK, HD), BF16),
            pltpu.VMEM((4, HPD, HD, BLK), BF16),
            pltpu.VMEM((4, HPD, 1, BLK), F32),
            pltpu.VMEM((NB * BLK, HD), F32),
            pltpu.VMEM((NB * BLK, HD), F32),
            pltpu.VMEM((HPD, HD, BLK), F32),
        ],
        compiler_params=pltpu.CompilerParams(vmem_limit_bytes=VMEM_LIMIT),
        cost_estimate=pl.CostEstimate(flops=25 * 10**9, bytes_accessed=16 << 20, transcendentals=10**7),
        name="attention_backward",
    )(scal, *qs, *us, *kp, *vp, w, out, lse, err)


def send(x, move):
    pairs = []
    for b in range(NB):
        o, z, y = move(b // 16, b // 4 % 4, b % 4)
        pairs.append((b, 16 * o + 4 * (z % 4) + y % 4))
    return lax.ppermute(x, CTX, pairs)


def swap(x, k):
    def move(o, z, y):
        if k & 1:
            z, y = 3 - z, 3 - y
        return (o ^ (k >> 1), z, y)

    return send(x, move)


def from_z(x, d):
    return send(x, lambda o, z, y: (o, z - d, y))


def from_y(x, d):
    return send(x, lambda o, z, y: (o, z, y - d))


def quarter(x, index):
    return lax.dynamic_slice_in_dim(x, index * WIDTH, WIDTH, 1)


def total_of(parts):
    return functools.reduce(jnp.add, [x.astype(F32) for x in parts])


def local(queries, keys, values, segment_ids, value_weight, targets, upstream):
    o = lax.axis_index("outer")
    i = lax.axis_index("inner")
    head = lax.axis_index("head")
    z, y = i // 4, i % 4
    member = 2 * o + i // 8

    below = jnp.sum(
        segment_ids[:, None] < jnp.arange(HD, dtype=jnp.int32)[None, :], 0, dtype=jnp.int32
    )
    below = jnp.where(jnp.arange(HD) < 8, below, 0).astype(F32).astype(BF16)
    pad = jnp.concatenate([below[None, :], jnp.zeros((PAD - 1, HD), BF16)], 0)

    def packed(index):
        k = lax.dynamic_slice_in_dim(keys, index * HD, HD, 1)
        v = lax.dynamic_slice_in_dim(values, index * HD, HD, 1)
        return jnp.concatenate([k, pad, v], 0)

    mine = packed(o)
    other = swap(packed(1 - o), 2)
    pair = jnp.stack([jnp.where(o == 0, mine, other), jnp.where(o == 0, other, mine)])
    k_pair, v_pair = pair[:, : BLK + PAD], pair[:, BLK + PAD:]
    k_line = jnp.stack([k_pair] + [from_z(k_pair, d) for d in (1, 2, 3)])
    v_line = jnp.stack([v_pair] + [from_y(v_pair, d) for d in (1, 2, 3)])
    kp = [k_line] + [from_y(k_line, d) for d in (1, 2, 3)]
    vp = [v_line] + [from_z(v_line, d) for d in (1, 2, 3)]
    starts = jnp.sum(total_of([k[:, :, BLK, :8] for k in kp]), (0, 1)).astype(jnp.int32)

    qs = [quarter(queries, member)] + [swap(quarter(queries, member ^ k), k) for k in (1, 2, 3)]
    us = [quarter(upstream, member)] + [swap(quarter(upstream, member ^ k), k) for k in (1, 2, 3)]
    bases = [
        BLK * (16 * (o ^ (k >> 1)) + (15 - i if k & 1 else i)) for k in range(4)
    ]
    scal = jnp.concatenate(
        [starts, jnp.stack(bases + [z, y, z, y]).astype(jnp.int32)]
    )
    w = jnp.broadcast_to(
        lax.dynamic_slice_in_dim(value_weight, member * WIDTH, WIDTH, 0)[:, None], (WIDTH, HD)
    )

    out, lse, critic = forward(scal, qs, kp, vp, w)

    critic = critic[:, 0, :]
    critic = critic - jnp.concatenate(
        [jnp.where(head == 0, targets, 0.0)[None, :], jnp.zeros((3, BLK), F32)], 0
    )
    critic = lax.psum(critic, "head")
    err = critic
    for k in (1, 2, 3):
        got = swap(critic, k)
        err = err + jnp.stack([got[p ^ k] for p in range(4)])
    value_error = err[0]

    dq, *grads, readout = backward(scal, qs, us, kp, vp, w, out, lse, err[:, None, :])
    dk, dv = grads[:4], grads[4:]

    got = [dq[0]] + [swap(dq[k], k) for k in (1, 2, 3)]
    query_grad = jnp.concatenate(
        [
            jnp.select([member == m for m in range(3)], [got[c ^ m] for m in range(3)], got[c ^ 3])
            for c in range(4)
        ],
        1,
    )

    dk_line = total_of([dk[0]] + [send(dk[d], lambda o, z, y, d=d: (o, z, y + d)) for d in (1, 2, 3)])
    dv_line = total_of([dv[0]] + [send(dv[d], lambda o, z, y, d=d: (o, z + d, y)) for d in (1, 2, 3)])
    dk_line, dv_line = dk_line.astype(BF16), dv_line.astype(BF16)
    dk_pair = total_of(
        [dk_line[0]] + [send(dk_line[d], lambda o, z, y, d=d: (o, z + d, y)) for d in (1, 2, 3)]
    )
    dv_pair = total_of(
        [dv_line[0]] + [send(dv_line[d], lambda o, z, y, d=d: (o, z, y + d)) for d in (1, 2, 3)]
    )
    pair = jnp.concatenate([dk_pair, dv_pair], 2).astype(BF16)
    mine = jnp.where(o == 0, pair[0], pair[1])
    other = swap(jnp.where(o == 0, pair[1], pair[0]), 2)
    low, high = jnp.where(o == 0, mine, other), jnp.where(o == 0, other, mine)
    key_grad = jnp.concatenate([low[:, :HD], high[:, :HD]], 1)
    value_grad = jnp.concatenate([low[:, HD:], high[:, HD:]], 1)

    spread = lax.dynamic_update_slice_in_dim(
        jnp.zeros((4, WIDTH), F32), readout[:, 0][None, :], member, 0
    )
    line = total_of([spread] + [from_y(spread, d) for d in (1, 2, 3)])
    line = total_of([line] + [from_z(line, d) for d in (1, 2, 3)])
    readout_grad = (line + swap(line, 2)).reshape(-1)
    return (query_grad, key_grad, value_grad, value_error, readout_grad)


def solution(mesh):
    return jax.shard_map(
        local,
        mesh=mesh,
        in_specs=(
            P(CTX, "head"),
            P(CTX, "head"),
            P(CTX, "head"),
            P(CTX),
            P("head"),
            P(CTX),
            P(CTX, "head"),
        ),
        out_specs=(
            P(CTX, "head"),
            P(CTX, "head"),
            P(CTX, "head"),
            P(CTX),
            P("head"),
        ),
        check_vma=False,
    )
```

```python
import functools
import math

import jax
import jax.numpy as jnp
from jax import lax
from jax.experimental import pallas as pl
from jax.experimental.pallas import tpu as pltpu
from jax.sharding import PartitionSpec as P

HD = 128
BLK = 256
NB = 32
HPD = 4
WIDTH = HPD * HD
PAD = 16
LINE = 8 * HD
TILE = 4
SCALE = HD ** (-0.5)
SCALE2 = SCALE * math.log2(math.e)
NEG = -1e30
CTX = ("outer", "inner")
NT = (((1,), (1,)), ((), ()))
F32 = jnp.float32
BF16 = jnp.bfloat16
VMEM_LIMIT = 52 * 1024 * 1024


def dot(a, b):
    return jnp.dot(a, b, preferred_element_type=F32)


def dot_nt(a, b):
    return lax.dot_general(a, b, NT, preferred_element_type=F32)


def rows(b, n=1):
    return pl.ds(pl.multiple_of(b * BLK, BLK), n * BLK)


def block_of(scal, o, dz, dy):
    z = (scal[12] + dz) & 3
    y = (scal[13] + dy) & 3
    return 16 * o + 4 * z + y


def place(scal, pieces, z_first, put):
    for far in range(4):
        for near in range(4):
            for o in range(2):
                dz, dy = (near, far) if z_first else (far, near)
                put(block_of(scal, 0, dz, dy), o, pieces[far][near, o, :BLK, :])


def start_of(scal, pos):
    lo = jnp.zeros_like(pos)
    for v in range(1, 8):
        lo = jnp.maximum(lo, jnp.where(pos >= scal[v], scal[v], 0))
    return lo


def allowed_of(scal, base, kb):
    query_pos = base + lax.broadcasted_iota(jnp.int32, (1, BLK), 1)
    lo = start_of(scal, query_pos)
    key_pos = kb * BLK + lax.broadcasted_iota(jnp.int32, (BLK, BLK), 0)
    return (key_pos <= query_pos) & (key_pos >= lo)


def sweep(scal, base, low, high, tile, body):
    diag = base // BLK
    first = start_of(scal, base) // BLK
    full = jnp.minimum((start_of(scal, base + BLK - 1) + BLK - 1) // BLK, diag)
    stop = jnp.clip(diag, low, high)
    full = jnp.clip(full, low, stop)
    first = jnp.clip(first, low, full)

    @pl.when((diag >= low) & (diag < high))
    def _():
        body(diag, 1, True)

    def masked(kb, c):
        body(kb, 1, True)
        return c

    def plain(t, c):
        body(full + tile * t, tile, False)
        return c

    def single(kb, c):
        body(kb, 1, False)
        return c

    count = (stop - full) // tile
    lax.fori_loop(first, full, masked, 0)
    lax.fori_loop(0, count, plain, 0)
    lax.fori_loop(full + tile * count, stop, single, 0)


def largest_norm(blocks):
    ones = jnp.ones((8, HD), BF16)
    most = jnp.zeros((8, BLK), F32)
    for x in blocks:
        most = jnp.maximum(most, dot_nt(ones, x * x))
    return jnp.max(most) * 1.02


def forward_kernel(
    scal, q0, q1, q2, q3, k0, k1, k2, k3, v0, v1, v2, v3, w_ref,
    out_ref, lse_ref, critic_ref, qt_ref,
    k_all, vt_all, qt_all, acc, top, tot, flag,
):
    p = pl.program_id(0)

    @pl.when(p == 0)
    def _():
        norms = []
        for piece, q in enumerate((q0, q1, q2, q3)):
            for h in range(HPD):
                x = q[:, h * HD:(h + 1) * HD]
                qt_all[piece, h] = x.T
                norms.append(x)
        query_norm = largest_norm(norms)
        norms = []

        def put_k(b, o, blk):
            k_all[rows(b + 16 * o), :] = blk
            norms.append(blk)

        def put_v(b, o, blk):
            vt_all[b + 16 * o] = blk.T

        place(scal, (k0, k1, k2, k3), True, put_k)
        place(scal, (v0, v1, v2, v3), False, put_v)
        small = query_norm * largest_norm(norms) * SCALE2 * SCALE2 <= 3600.0
        flag[0] = small.astype(jnp.int32)

    small = flag[0] == 1
    base = scal[8 + p]
    tot[...] = jnp.zeros_like(tot)
    acc[...] = jnp.zeros_like(acc)
    for h in range(HPD):
        qt_ref[0, h] = qt_all[p, h]

    def values_of(kb, n):
        return jnp.concatenate([vt_all[kb + t] for t in range(n)], 1)

    def bounded(kb, n, masked):
        k_blk = k_all[rows(kb, n), :]
        vt_blk = values_of(kb, n)
        if masked:
            allowed = allowed_of(scal, base, kb)
        ss = [dot(k_blk, qt_all[p, h]) for h in range(HPD)]
        probs = [jnp.exp2(s * SCALE2) for s in ss]
        if masked:
            probs = [jnp.where(allowed, x, 0.0) for x in probs]
        pv = [dot(vt_blk, x.astype(BF16)) for x in probs]
        tots = [tot[h] + jnp.sum(probs[h], 0, keepdims=True) for h in range(HPD)]
        accs = [acc[h] + pv[h] for h in range(HPD)]
        for h in range(HPD):
            tot[h] = tots[h]
            acc[h] = accs[h]

    def general(kb, n, masked):
        k_blk = k_all[rows(kb, n), :]
        vt_blk = values_of(kb, n)
        ss = [dot(k_blk, qt_all[p, h]) for h in range(HPD)]
        if masked:
            allowed = allowed_of(scal, base, kb)
            ss = [jnp.where(allowed, s, NEG) for s in ss]
        olds = [top[h] for h in range(HPD)]
        news = [jnp.maximum(olds[h], jnp.max(ss[h], 0, keepdims=True)) for h in range(HPD)]
        probs = [jnp.exp2(ss[h] * SCALE2 - news[h] * SCALE2) for h in range(HPD)]
        fades = [jnp.exp2((olds[h] - news[h]) * SCALE2) for h in range(HPD)]
        pv = [dot(vt_blk, x.astype(BF16)) for x in probs]
        tots = [tot[h] * fades[h] + jnp.sum(probs[h], 0, keepdims=True) for h in range(HPD)]
        accs = [acc[h] * fades[h] + pv[h] for h in range(HPD)]
        for h in range(HPD):
            top[h] = news[h]
            tot[h] = tots[h]
            acc[h] = accs[h]

    @pl.when(small)
    def _():
        top[...] = jnp.zeros_like(top)
        sweep(scal, base, 0, NB, TILE, bounded)

    @pl.when(jnp.logical_not(small))
    def _():
        top[...] = jnp.full_like(top, NEG)
        sweep(scal, base, 0, NB, TILE, general)

    critic = jnp.zeros((1, BLK), F32)
    for h in range(HPD):
        total = tot[h]
        out = (acc[h] / total).astype(BF16)
        out_ref[0, h] = out
        lse_ref[0, h] = top[h] * SCALE2 + jnp.log2(total)
        w = w_ref[h * HD:(h + 1) * HD, :]
        critic += jnp.sum(out.astype(F32) * jnp.concatenate([w, w], 1), 0, keepdims=True)
    critic_ref[0] = critic


def prepare_kernel(
    scal, q0, q1, q2, q3, u0, u1, u2, u3, k0, k1, k2, k3, v0, v1, v2, v3,
    q_ref, ut_ref, k_low, k_high, kt_low, kt_high, vt_low, vt_high,
):
    for p, (q, u) in enumerate(((q0, u0), (q1, u1), (q2, u2), (q3, u3))):
        q_ref[p] = q[...]
        for h in range(HPD):
            ut_ref[p, h] = u[:, h * HD:(h + 1) * HD].T

    def put_k(b, o, blk):
        (k_low, k_high)[o][rows(b), :] = blk
        (kt_low, kt_high)[o][b] = blk.T

    def put_v(b, o, blk):
        (vt_low, vt_high)[o][b] = blk.T

    place(scal, (k0, k1, k2, k3), True, put_k)
    place(scal, (v0, v1, v2, v3), False, put_v)


def spread(row):
    return jnp.broadcast_to(row, (HD, BLK)).T


def allowed_by_row(scal, base, kb):
    query_pos = base + lax.broadcasted_iota(jnp.int32, (BLK, HD), 0)
    lo = start_of(scal, query_pos)
    key_pos = kb * BLK + lax.broadcasted_iota(jnp.int32, (BLK, HD), 1)
    halves = [(x <= query_pos) & (x >= lo) for x in (key_pos, key_pos + HD)]
    return halves


def gradients(scal, low, high, q_ref, qt_ref, k_ref, kt_ref, vt_ref, do_s, dot_ref, lse_s, delta_s, dkt, dvt, dq):
    base = scal[8 + pl.program_id(0)]

    def body(kb, n, masked):
        at = kb - low
        k_blk = k_ref[rows(at, n), :]
        kt_blk = jnp.concatenate([kt_ref[at + t] for t in range(n)], 1)
        vt_blk = jnp.concatenate([vt_ref[at + t] for t in range(n)], 1)
        ss = [dot(q_ref[0, :, h * HD:(h + 1) * HD], kt_blk) for h in range(HPD)]
        dps = [dot(do_s[h], vt_blk) for h in range(HPD)]
        lses = [jnp.concatenate([lse_s[h]] * (2 * n), 1) for h in range(HPD)]
        deltas = [jnp.concatenate([delta_s[h]] * (2 * n), 1) for h in range(HPD)]
        probs = [jnp.exp2(ss[h] * SCALE2 - lses[h]) for h in range(HPD)]
        if masked:
            left, right = allowed_by_row(scal, base, kb)
            probs = [
                jnp.concatenate([jnp.where(left, x[:, :HD], 0.0), jnp.where(right, x[:, HD:], 0.0)], 1)
                for x in probs
            ]
        dls = [(probs[h] * (dps[h] - deltas[h])).astype(BF16) for h in range(HPD)]
        dv = sum(dot(dot_ref[0, h], probs[h].astype(BF16)) for h in range(HPD))
        dk = sum(dot(qt_ref[0, h], dls[h]) for h in range(HPD))
        upd = [dq[h] + dot(dls[h], k_blk) for h in range(HPD)]
        for h in range(HPD):
            dq[h] = upd[h]
        for t in range(n):
            span = slice(t * BLK, (t + 1) * BLK)
            dkt[at + t] += dk[:, span]
            dvt[at + t] += dv[:, span]

    sweep(scal, base, low, high, TILE, body)


def write_lines(scal, dkt, dvt, lines):
    for dy, line in enumerate(lines):
        for dz in range(4):
            b = block_of(scal, 0, dz, dy)
            line[2 * dz * HD:(2 * dz + 1) * HD, :] = (dkt[b] * SCALE).astype(BF16)
            line[(2 * dz + 1) * HD:(2 * dz + 2) * HD, :] = dvt[b].astype(BF16)


def upper_kernel(
    scal, q_ref, ut_ref, qt_ref, k_ref, kt_ref, vt_ref, w_ref, out_ref, lse_ref, err_ref,
    part_ref, dot_ref, delta_ref, line0, line1, line2, line3,
    dkt, dvt, dq, do_s, lse_s, delta_s, readout, readout_all,
):
    p = pl.program_id(0)

    @pl.when(p == 0)
    def _():
        dkt[...] = jnp.zeros_like(dkt)
        dvt[...] = jnp.zeros_like(dvt)
        readout[...] = jnp.zeros_like(readout)

    dq[...] = jnp.zeros_like(dq)
    err = err_ref[0]
    for h in range(HPD):
        w = w_ref[h * HD:(h + 1) * HD, :]
        w = jnp.concatenate([w, w], 1)
        out = out_ref[0, h].astype(F32)
        dout = (err * w + ut_ref[0, h].astype(F32)).astype(BF16)
        delta = jnp.sum(dout.astype(F32) * out, 0, keepdims=True)
        dot_ref[0, h] = dout
        delta_ref[0, h] = delta
        do_s[h] = dout.T
        delta_s[h] = spread(delta)
        lse_s[h] = spread(lse_ref[0, h])
        readout[h] += err * out
    gradients(
        scal, NB // 2, NB, q_ref, qt_ref, k_ref, kt_ref, vt_ref, do_s, dot_ref, lse_s, delta_s, dkt, dvt, dq
    )
    part_ref[0] = dq[...].astype(BF16)

    @pl.when(p == 3)
    def _():
        readout_all[...] = jnp.zeros_like(readout_all)
        lanes = [jnp.sum(readout[h].T, 0, keepdims=True) for h in range(HPD)]
        for r in range(2):
            readout_all[pl.ds(2 * scal[14] + r, 1), :] = jnp.concatenate(lanes[2 * r:2 * r + 2], 1)
        high = readout_all[...].astype(BF16).astype(F32)
        tail = jnp.concatenate([high, readout_all[...] - high], 0).astype(BF16)
        lines = (line0, line1, line2, line3)
        write_lines(scal, dkt, dvt, lines)
        for line in lines:
            line[LINE:, :] = tail


def lower_kernel(
    scal, q_ref, qt_ref, k_ref, kt_ref, vt_ref, dot_ref, lse_ref, delta_ref, part_ref,
    dq_ref, line0, line1, line2, line3,
    dkt, dvt, dq, do_s, lse_s, delta_s,
):
    p = pl.program_id(0)

    @pl.when(p == 0)
    def _():
        dkt[...] = jnp.zeros_like(dkt)
        dvt[...] = jnp.zeros_like(dvt)

    for h in range(HPD):
        do_s[h] = dot_ref[0, h].T
        delta_s[h] = spread(delta_ref[0, h])
        lse_s[h] = spread(lse_ref[0, h])
    dq[...] = part_ref[0].astype(F32)
    gradients(
        scal, 0, NB // 2, q_ref, qt_ref, k_ref, kt_ref, vt_ref, do_s, dot_ref, lse_s, delta_s, dkt, dvt, dq
    )
    for h in range(HPD):
        dq_ref[0, :, h * HD:(h + 1) * HD] = (dq[h] * SCALE).astype(BF16)

    @pl.when(p == 3)
    def _():
        write_lines(scal, dkt, dvt, (line0, line1, line2, line3))


SMEM_SPEC = pl.BlockSpec(memory_space=pltpu.SMEM)
VMEM_SPEC = pl.BlockSpec(memory_space=pltpu.VMEM)


def by_piece(shape):
    return pl.BlockSpec((1, *shape[1:]), lambda p: (p,) + (0,) * (len(shape) - 1))


def call(kernel, name, shapes, scratch, flops, split, *args):
    shapes = [jax.ShapeDtypeStruct(shape, kind) for shape, kind in shapes]
    every = [*args, *shapes]
    specs = [SMEM_SPEC] + [
        by_piece(every[t].shape) if t in split else VMEM_SPEC for t in range(1, len(every))
    ]
    return pl.pallas_call(
        kernel,
        grid=(4,) if split else (),
        out_shape=tuple(shapes),
        in_specs=specs[:len(args)],
        out_specs=tuple(specs[len(args):]),
        scratch_shapes=[
            pltpu.SMEM((1,), jnp.int32) if kind is None else pltpu.VMEM(shape, kind) for shape, kind in scratch
        ],
        compiler_params=pltpu.CompilerParams(vmem_limit_bytes=VMEM_LIMIT),
        cost_estimate=pl.CostEstimate(flops=flops, bytes_accessed=8 << 20, transcendentals=10**6),
        name=name,
    )(*args)


HEADS = (4, HPD, HD, BLK)
STATS = (4, HPD, 1, BLK)
PIECES = (4, BLK, WIDTH)
COLUMNS = ((HPD, BLK, HD), F32)
HALF = ((NB // 2 * BLK, HD), BF16)
HALF_T = ((NB // 2, HD, BLK), BF16)
SUMS = ((NB // 2, HD, BLK), F32)


def forward(scal, qs, kp, vp, w):
    return call(
        forward_kernel, "attention_forward",
        [(HEADS, BF16), (STATS, F32), ((4, 1, BLK), F32), (HEADS, BF16)],
        [
            ((NB * BLK, HD), BF16), ((NB, HD, BLK), BF16), (HEADS, BF16),
            (HEADS[1:], F32), (STATS[1:], F32), (STATS[1:], F32), ((1,), None),
        ],
        9 * 10**9, (14, 15, 16, 17), scal, *qs, *kp, *vp, w,
    )


def prepare(scal, qs, us, kp, vp):
    return call(
        prepare_kernel, "prepare_backward",
        [(PIECES, BF16), (HEADS, BF16), HALF, HALF, HALF_T, HALF_T, HALF_T, HALF_T],
        [], 10**8, (), scal, *qs, *us, *kp, *vp,
    )


def upper(scal, q, ut, qt, k, kt, vt, w, out, lse, err):
    return call(
        upper_kernel, "attention_upper",
        [((4, HPD, BLK, HD), BF16), (HEADS, BF16), (STATS, F32)]
        + [((LINE + 16, BLK), BF16)] * 4,
        [SUMS, SUMS, COLUMNS, ((HPD, BLK, HD), BF16), COLUMNS, COLUMNS, (HEADS[1:], F32), ((8, BLK), F32)],
        8 * 10**9, (1, 2, 3, 8, 9, 10, 11, 12, 13), scal, q, ut, qt, k, kt, vt, w, out, lse, err,
    )


def lower(scal, q, qt, k, kt, vt, dout, lse, delta, part):
    return call(
        lower_kernel, "attention_lower",
        [(PIECES, BF16)] + [((LINE, BLK), BF16)] * 4,
        [SUMS, SUMS, COLUMNS, ((HPD, BLK, HD), BF16), COLUMNS, COLUMNS],
        16 * 10**9, (1, 2, 6, 7, 8, 9, 10), scal, q, qt, k, kt, vt, dout, lse, delta, part,
    )


def send(x, move):
    pairs = []
    for b in range(NB):
        o, z, y = move(b // 16, b // 4 % 4, b % 4)
        pairs.append((b, 16 * o + 4 * (z % 4) + y % 4))
    return lax.ppermute(x, CTX, pairs)


def swap(x, k):
    def move(o, z, y):
        if k & 1:
            z, y = 3 - z, 3 - y
        return (o ^ (k >> 1), z, y)

    return send(x, move)


def from_z(x, d):
    return send(x, lambda o, z, y: (o, z - d, y))


def from_y(x, d):
    return send(x, lambda o, z, y: (o, z, y - d))


def to_z(x, d):
    return send(x, lambda o, z, y: (o, z + d, y))


def to_y(x, d):
    return send(x, lambda o, z, y: (o, z, y + d))


def quarter(x, index):
    return lax.dynamic_slice_in_dim(x, index * WIDTH, WIDTH, 1)


def halves(x):
    high = lax.reduce_precision(x, 8, 7)
    return jnp.concatenate([high, x - high], 0).astype(BF16)


def joined(x):
    return x[:8] + x[8:]


def total_of(parts):
    return functools.reduce(jnp.add, [x.astype(F32) for x in parts])


def local(queries, keys, values, segment_ids, value_weight, targets, upstream):
    o = lax.axis_index("outer")
    i = lax.axis_index("inner")
    head = lax.axis_index("head")
    z, y = i // 4, i % 4
    member = 2 * o + i // 8

    below = jnp.sum(
        segment_ids[:, None] < jnp.arange(HD, dtype=jnp.int32)[None, :], 0, dtype=jnp.int32
    )
    below = jnp.where(jnp.arange(HD) < 8, below, 0).astype(F32).astype(BF16)
    pad = jnp.concatenate([below[None, :], jnp.zeros((PAD - 1, HD), BF16)], 0)

    def packed(index):
        k = lax.dynamic_slice_in_dim(keys, index * HD, HD, 1)
        v = lax.dynamic_slice_in_dim(values, index * HD, HD, 1)
        return jnp.concatenate([k, pad, v], 0)

    mine = packed(o)
    other = packed(1 - o).reshape(-1, WIDTH)
    qs = [quarter(queries, member)] + [quarter(queries, member ^ k) for k in (1, 2, 3)]
    qs[2] = jnp.concatenate([qs[2], other], 0)
    qs[1:] = [swap(qs[k], k) for k in (1, 2, 3)]
    qs[2], other = qs[2][:BLK], qs[2][BLK:].reshape(2 * BLK + PAD, HD)
    pair = jnp.stack([jnp.where(o == 0, mine, other), jnp.where(o == 0, other, mine)])
    k_pair, v_pair = pair[:, :BLK + PAD], pair[:, BLK + PAD:]
    k_pair, v_pair, qs = lax.optimization_barrier((k_pair, v_pair, qs))
    k_line = jnp.stack([k_pair] + [from_z(k_pair, d) for d in (1, 2, 3)])
    v_line = jnp.stack([v_pair] + [from_y(v_pair, d) for d in (1, 2, 3)])
    k_line, v_line = lax.optimization_barrier((k_line, v_line))
    kp = [k_line] + [from_y(k_line, d) for d in (1, 2, 3)]
    vp = [v_line] + [from_z(v_line, d) for d in (1, 2, 3)]
    kp, vp, upstream = lax.optimization_barrier((kp, vp, upstream))
    us = [quarter(upstream, member)] + [swap(quarter(upstream, member ^ k), k) for k in (1, 2, 3)]
    starts = jnp.sum(total_of([k[:, :, BLK, :8] for k in kp]), (0, 1)).astype(jnp.int32)
    bases = [
        BLK * (16 * (o ^ (k >> 1)) + (15 - i if k & 1 else i)) for k in range(4)
    ]
    scal = jnp.concatenate(
        [starts, jnp.stack(bases + [z, y, member, member]).astype(jnp.int32)]
    )
    w = jnp.broadcast_to(
        lax.dynamic_slice_in_dim(value_weight, member * WIDTH, WIDTH, 0)[:, None], (WIDTH, HD)
    )

    out, lse, critic, qt = forward(scal, qs, kp, vp, w)

    critic, us = lax.optimization_barrier((critic, us))
    q, ut, *halved = prepare(scal, qs, us, kp, vp)
    keys_low, keys_high = halved[0::2], halved[1::2]
    critic = critic[:, 0, :]
    critic = critic - jnp.concatenate(
        [jnp.where(head == 0, targets, 0.0)[None, :], jnp.zeros((3, BLK), F32)], 0
    )
    critic = lax.psum(critic, "head")
    err = critic
    for k in (1, 2, 3):
        got = swap(critic, k)
        err = err + jnp.stack([got[p ^ k] for p in range(4)])
    value_error = err[0]

    part, dout, delta, *grads = upper(scal, q, ut, qt, *keys_high, w, out, lse, err[:, None, :])
    high = [grads[0]] + [to_y(grads[d], d) for d in (1, 2, 3)]
    dq, *grads = lower(scal, q, qt, *keys_low, dout, lse, delta, part)
    high, grads = lax.optimization_barrier((high, grads))
    low = [grads[0]] + [to_y(grads[d], d) for d in (1, 2, 3)]
    high = total_of(high)
    tail = halves(joined(high[LINE:]))
    high = high[:LINE].astype(BF16).reshape(4, 2 * HD, BLK)
    low = total_of(low).astype(BF16).reshape(4, 2 * HD, BLK)
    both = [jnp.concatenate([low[d], high[d], tail], 0) for d in range(4)]
    both = total_of([both[0]] + [to_z(both[d], d) for d in (1, 2, 3)])
    readout = joined(both[4 * HD:])
    low, high = both[:2 * HD].astype(BF16), both[2 * HD:4 * HD].astype(BF16)
    mine, other = jnp.where(o == 0, low, high), jnp.where(o == 0, high, low)
    other = swap(jnp.concatenate([other, halves(readout)], 0), 2)
    readout_grad = (readout + joined(other[2 * HD:].astype(F32))).reshape(-1)
    other = other[:2 * HD]
    first, second = jnp.where(o == 0, mine, other), jnp.where(o == 0, other, mine)
    key_grad = jnp.concatenate([first[:HD], second[:HD]], 0).T
    value_grad = jnp.concatenate([first[HD:], second[HD:]], 0).T

    got = [dq[0]] + [swap(dq[k], k) for k in (1, 2, 3)]
    query_grad = jnp.concatenate(
        [
            jnp.select([member == m for m in range(3)], [got[c ^ m] for m in range(3)], got[c ^ 3])
            for c in range(4)
        ],
        1,
    )
    return (query_grad, key_grad, value_grad, value_error, readout_grad)


def solution(mesh):
    return jax.shard_map(
        local,
        mesh=mesh,
        in_specs=(
            P(CTX, "head"),
            P(CTX, "head"),
            P(CTX, "head"),
            P(CTX),
            P("head"),
            P(CTX),
            P(CTX, "head"),
        ),
        out_specs=(
            P(CTX, "head"),
            P(CTX, "head"),
            P(CTX, "head"),
            P(CTX),
            P("head"),
        ),
        check_vma=False,
    )
```

```python
import functools
import math

import jax
import jax.numpy as jnp
from jax import lax
from jax.experimental import pallas as pl
from jax.experimental.pallas import tpu as pltpu
from jax.sharding import PartitionSpec as P

HD = 128
BLK = 256
NB = 32
HPD = 4
WIDTH = HPD * HD
PAD = 16
LINE = 4 * HD
TILE = 4
SCALE = HD ** (-0.5)
SCALE2 = SCALE * math.log2(math.e)
NEG = -1e30
CTX = ("outer", "zh", "zl", "y")
GROUP = ("outer", "zh")
NT = (((1,), (1,)), ((), ()))
F32 = jnp.float32
BF16 = jnp.bfloat16
VMEM_LIMIT = 52 * 1024 * 1024


def dot(a, b):
    return jnp.dot(a, b, preferred_element_type=F32)


def dot_nt(a, b):
    return lax.dot_general(a, b, NT, preferred_element_type=F32)


def rows(b, n=1):
    return pl.ds(pl.multiple_of(b * BLK, BLK), n * BLK)


def block_of(scal, o, dz, dy):
    z = (scal[12] + dz) & 3
    y = (scal[13] + dy) & 3
    return 16 * o + 4 * z + y


def place(scal, pieces, z_first, put):
    for far in range(4):
        for near in range(4):
            for o in range(2):
                dz, dy = (near, far) if z_first else (far, near)
                put(block_of(scal, 0, dz, dy), o, pieces[far][near, o, :BLK, :])


def start_of(scal, pos):
    lo = jnp.zeros_like(pos)
    for v in range(1, 8):
        lo = jnp.maximum(lo, jnp.where(pos >= scal[v], scal[v], 0))
    return lo


def allowed_of(scal, base, kb):
    query_pos = base + lax.broadcasted_iota(jnp.int32, (1, BLK), 1)
    lo = start_of(scal, query_pos)
    key_pos = kb * BLK + lax.broadcasted_iota(jnp.int32, (BLK, BLK), 0)
    return (key_pos <= query_pos) & (key_pos >= lo)


def sweep(scal, base, low, high, tile, body):
    diag = base // BLK
    first = start_of(scal, base) // BLK
    full = jnp.minimum((start_of(scal, base + BLK - 1) + BLK - 1) // BLK, diag)
    stop = jnp.clip(diag, low, high)
    full = jnp.clip(full, low, stop)
    first = jnp.clip(first, low, full)

    @pl.when((diag >= low) & (diag < high))
    def _():
        body(diag, 1, True)

    def masked(kb, c):
        body(kb, 1, True)
        return c

    def plain(t, c):
        body(full + tile * t, tile, False)
        return c

    def single(kb, c):
        body(kb, 1, False)
        return c

    count = (stop - full) // tile
    lax.fori_loop(first, full, masked, 0)
    lax.fori_loop(0, count, plain, 0)
    lax.fori_loop(full + tile * count, stop, single, 0)


def largest_norm(blocks):
    ones = jnp.ones((8, HD), BF16)
    most = jnp.zeros((8, BLK), F32)
    for x in blocks:
        most = jnp.maximum(most, dot_nt(ones, x * x))
    return jnp.max(most) * 1.02


def forward_kernel(
    scal, q_ref, k0, k1, k2, k3, v0, v1, v2, v3, w_ref,
    out_ref, lse_ref, critic_ref, qt_ref,
    k_all, vt_all, qt_all, acc, top, tot, flag,
):
    p = pl.program_id(0)

    @pl.when(p == 0)
    def _():
        norms = []
        for piece in range(4):
            for h in range(HPD):
                x = q_ref[piece, :, h * HD:(h + 1) * HD]
                qt_all[piece, h] = x.T
                norms.append(x)
        query_norm = largest_norm(norms)
        norms = []

        def put_k(b, o, blk):
            k_all[rows(b + 16 * o), :] = blk
            norms.append(blk)

        def put_v(b, o, blk):
            vt_all[b + 16 * o] = blk.T

        place(scal, (k0, k1, k2, k3), True, put_k)
        place(scal, (v0, v1, v2, v3), False, put_v)
        small = query_norm * largest_norm(norms) * SCALE2 * SCALE2 <= 3600.0
        flag[0] = small.astype(jnp.int32)

    small = flag[0] == 1
    base = scal[8 + p]
    tot[...] = jnp.zeros_like(tot)
    acc[...] = jnp.zeros_like(acc)
    for h in range(HPD):
        qt_ref[0, h] = qt_all[p, h]

    def values_of(kb, n):
        return jnp.concatenate([vt_all[kb + t] for t in range(n)], 1)

    def bounded(kb, n, masked):
        k_blk = k_all[rows(kb, n), :]
        vt_blk = values_of(kb, n)
        if masked:
            allowed = allowed_of(scal, base, kb)
        ss = [dot(k_blk, qt_all[p, h]) for h in range(HPD)]
        probs = [jnp.exp2(s * SCALE2) for s in ss]
        if masked:
            probs = [jnp.where(allowed, x, 0.0) for x in probs]
        pv = [dot(vt_blk, x.astype(BF16)) for x in probs]
        tots = [tot[h] + jnp.sum(probs[h], 0, keepdims=True) for h in range(HPD)]
        accs = [acc[h] + pv[h] for h in range(HPD)]
        for h in range(HPD):
            tot[h] = tots[h]
            acc[h] = accs[h]

    def general(kb, n, masked):
        k_blk = k_all[rows(kb, n), :]
        vt_blk = values_of(kb, n)
        ss = [dot(k_blk, qt_all[p, h]) for h in range(HPD)]
        if masked:
            allowed = allowed_of(scal, base, kb)
            ss = [jnp.where(allowed, s, NEG) for s in ss]
        olds = [top[h] for h in range(HPD)]
        news = [jnp.maximum(olds[h], jnp.max(ss[h], 0, keepdims=True)) for h in range(HPD)]
        probs = [jnp.exp2(ss[h] * SCALE2 - news[h] * SCALE2) for h in range(HPD)]
        fades = [jnp.exp2((olds[h] - news[h]) * SCALE2) for h in range(HPD)]
        pv = [dot(vt_blk, x.astype(BF16)) for x in probs]
        tots = [tot[h] * fades[h] + jnp.sum(probs[h], 0, keepdims=True) for h in range(HPD)]
        accs = [acc[h] * fades[h] + pv[h] for h in range(HPD)]
        for h in range(HPD):
            top[h] = news[h]
            tot[h] = tots[h]
            acc[h] = accs[h]

    @pl.when(small)
    def _():
        top[...] = jnp.zeros_like(top)
        sweep(scal, base, 0, NB, TILE, bounded)

    @pl.when(jnp.logical_not(small))
    def _():
        top[...] = jnp.full_like(top, NEG)
        sweep(scal, base, 0, NB, TILE, general)

    critic = jnp.zeros((1, BLK), F32)
    for h in range(HPD):
        total = tot[h]
        out = (acc[h] / total).astype(BF16)
        out_ref[0, h] = out
        lse_ref[0, h] = top[h] * SCALE2 + jnp.log2(total)
        w = w_ref[h * HD:(h + 1) * HD, :]
        critic += jnp.sum(out.astype(F32) * jnp.concatenate([w, w], 1), 0, keepdims=True)
    critic_ref[0] = critic


def prepare_kernel(
    scal, u_ref, k0, k1, k2, k3, v0, v1, v2, v3,
    ut_ref, k_low, k_high, kt_low, kt_high, vt_low, vt_high,
):
    for p in range(4):
        for h in range(HPD):
            ut_ref[p, h] = u_ref[p, :, h * HD:(h + 1) * HD].T

    def put_k(b, o, blk):
        (k_low, k_high)[o][rows(b), :] = blk
        (kt_low, kt_high)[o][b] = blk.T

    def put_v(b, o, blk):
        (vt_low, vt_high)[o][b] = blk.T

    place(scal, (k0, k1, k2, k3), True, put_k)
    place(scal, (v0, v1, v2, v3), False, put_v)


def spread(row):
    return jnp.broadcast_to(row, (HD, BLK)).T


def allowed_by_row(scal, base, kb):
    query_pos = base + lax.broadcasted_iota(jnp.int32, (BLK, HD), 0)
    lo = start_of(scal, query_pos)
    key_pos = kb * BLK + lax.broadcasted_iota(jnp.int32, (BLK, HD), 1)
    halves = [(x <= query_pos) & (x >= lo) for x in (key_pos, key_pos + HD)]
    return halves


def gradients(scal, low, high, q_ref, qt_ref, k_ref, kt_ref, vt_ref, do_s, dot_ref, lse_s, delta_s, dkt, dvt, dq):
    base = scal[8 + pl.program_id(0)]

    def body(kb, n, masked):
        at = kb - low
        k_blk = k_ref[rows(at, n), :]
        kt_blk = jnp.concatenate([kt_ref[at + t] for t in range(n)], 1)
        vt_blk = jnp.concatenate([vt_ref[at + t] for t in range(n)], 1)
        ss = [dot(q_ref[0, :, h * HD:(h + 1) * HD], kt_blk) for h in range(HPD)]
        dps = [dot(do_s[h], vt_blk) for h in range(HPD)]
        lses = [jnp.concatenate([lse_s[h]] * (2 * n), 1) for h in range(HPD)]
        deltas = [jnp.concatenate([delta_s[h]] * (2 * n), 1) for h in range(HPD)]
        probs = [jnp.exp2(ss[h] * SCALE2 - lses[h]) for h in range(HPD)]
        if masked:
            left, right = allowed_by_row(scal, base, kb)
            probs = [
                jnp.concatenate([jnp.where(left, x[:, :HD], 0.0), jnp.where(right, x[:, HD:], 0.0)], 1)
                for x in probs
            ]
        dls = [(probs[h] * (dps[h] - deltas[h])).astype(BF16) for h in range(HPD)]
        dv = sum(dot(dot_ref[0, h], probs[h].astype(BF16)) for h in range(HPD))
        dk = sum(dot(qt_ref[0, h], dls[h]) for h in range(HPD))
        upd = [dq[h] + dot(dls[h], k_blk) for h in range(HPD)]
        for h in range(HPD):
            dq[h] = upd[h]
        for t in range(n):
            span = slice(t * BLK, (t + 1) * BLK)
            dkt[at + t] += dk[:, span]
            dvt[at + t] += dv[:, span]

    sweep(scal, base, low, high, TILE, body)


def key_sum(dkt, b):
    return (dkt[b] * SCALE).astype(BF16)


def value_sum(dvt, b):
    return dvt[b].astype(BF16)


def upper_kernel(
    scal, q_ref, ut_ref, qt_ref, k_ref, kt_ref, vt_ref, w_ref, out_ref, lse_ref, err_ref,
    part_ref, dot_ref, delta_ref, line0, line1, line2, line3,
    dkt, dvt, dq, do_s, lse_s, delta_s, readout, readout_all,
):
    p = pl.program_id(0)

    @pl.when(p == 0)
    def _():
        dkt[...] = jnp.zeros_like(dkt)
        dvt[...] = jnp.zeros_like(dvt)
        readout[...] = jnp.zeros_like(readout)

    dq[...] = jnp.zeros_like(dq)
    err = err_ref[0]
    for h in range(HPD):
        w = w_ref[h * HD:(h + 1) * HD, :]
        w = jnp.concatenate([w, w], 1)
        out = out_ref[0, h].astype(F32)
        dout = (err * w + ut_ref[0, h].astype(F32)).astype(BF16)
        delta = jnp.sum(dout.astype(F32) * out, 0, keepdims=True)
        dot_ref[0, h] = dout
        delta_ref[0, h] = delta
        do_s[h] = dout.T
        delta_s[h] = spread(delta)
        lse_s[h] = spread(lse_ref[0, h])
        readout[h] += err * out
    gradients(
        scal, NB // 2, NB, q_ref, qt_ref, k_ref, kt_ref, vt_ref, do_s, dot_ref, lse_s, delta_s, dkt, dvt, dq
    )
    part_ref[0] = dq[...].astype(BF16)

    @pl.when(p == 3)
    def _():
        readout_all[...] = jnp.zeros_like(readout_all)
        lanes = [jnp.sum(readout[h].T, 0, keepdims=True) for h in range(HPD)]
        for r in range(2):
            readout_all[pl.ds(2 * scal[14] + r, 1), :] = jnp.concatenate(lanes[2 * r:2 * r + 2], 1)
        high = readout_all[...].astype(BF16).astype(F32)
        tail = jnp.concatenate([high, readout_all[...] - high], 0).astype(BF16)
        for dy, line in enumerate((line0, line1, line2, line3)):
            for dz in range(4):
                b = block_of(scal, 0, dz, dy)
                line[2 * dz * HD:(2 * dz + 1) * HD, :] = key_sum(dkt, b)
                line[(2 * dz + 1) * HD:(2 * dz + 2) * HD, :] = value_sum(dvt, b)
            line[2 * LINE:, :] = tail


def lower_kernel(
    scal, q_ref, qt_ref, k_ref, kt_ref, vt_ref, dot_ref, lse_ref, delta_ref, part_ref,
    dq_ref, dk0, dk1, dk2, dk3, dv0, dv1, dv2, dv3,
    dkt, dvt, dq, do_s, lse_s, delta_s,
):
    p = pl.program_id(0)

    @pl.when(p == 0)
    def _():
        dkt[...] = jnp.zeros_like(dkt)
        dvt[...] = jnp.zeros_like(dvt)

    for h in range(HPD):
        do_s[h] = dot_ref[0, h].T
        delta_s[h] = spread(delta_ref[0, h])
        lse_s[h] = spread(lse_ref[0, h])
    dq[...] = part_ref[0].astype(F32)
    gradients(
        scal, 0, NB // 2, q_ref, qt_ref, k_ref, kt_ref, vt_ref, do_s, dot_ref, lse_s, delta_s, dkt, dvt, dq
    )
    for h in range(HPD):
        dq_ref[0, :, h * HD:(h + 1) * HD] = (dq[h] * SCALE).astype(BF16)

    @pl.when(p == 3)
    def _():
        for far, (dk, dv) in enumerate(((dk0, dv0), (dk1, dv1), (dk2, dv2), (dk3, dv3))):
            for near in range(4):
                span = slice(near * HD, (near + 1) * HD)
                dk[span, :] = key_sum(dkt, block_of(scal, 0, near, far))
                dv[span, :] = value_sum(dvt, block_of(scal, 0, far, near))


SMEM_SPEC = pl.BlockSpec(memory_space=pltpu.SMEM)
VMEM_SPEC = pl.BlockSpec(memory_space=pltpu.VMEM)


def by_piece(shape):
    return pl.BlockSpec((1, *shape[1:]), lambda p: (p,) + (0,) * (len(shape) - 1))


def call(kernel, name, shapes, scratch, flops, split, part, *args):
    shapes = [jax.ShapeDtypeStruct(shape, kind) for shape, kind in shapes]
    every = [*args, *shapes]
    specs = [SMEM_SPEC] + [
        by_piece(every[t].shape) if t in split else VMEM_SPEC for t in range(1, len(every))
    ]
    if part is not None:
        specs[1] = part
    return pl.pallas_call(
        kernel,
        grid=(4 if split else 1,),
        out_shape=tuple(shapes),
        in_specs=specs[:len(args)],
        out_specs=tuple(specs[len(args):]),
        scratch_shapes=[
            pltpu.SMEM((1,), jnp.int32) if kind is None else pltpu.VMEM(shape, kind) for shape, kind in scratch
        ],
        compiler_params=pltpu.CompilerParams(vmem_limit_bytes=VMEM_LIMIT),
        cost_estimate=pl.CostEstimate(flops=flops, bytes_accessed=8 << 20, transcendentals=10**6),
        name=name,
    )(*args)


ALL_QUERIES = pl.BlockSpec((4, BLK, WIDTH), lambda p: (0, 0, 0))
ALL_UPSTREAM = pl.BlockSpec((4, BLK, WIDTH), lambda p: (0, 1, 0))
ONE_QUERIES = pl.BlockSpec((1, BLK, WIDTH), lambda p: (p, 0, 0))
HEADS = (4, HPD, HD, BLK)
STATS = (4, HPD, 1, BLK)
PIECES = (4, BLK, WIDTH)
COLUMNS = ((HPD, BLK, HD), F32)
HALF = ((NB // 2 * BLK, HD), BF16)
HALF_T = ((NB // 2, HD, BLK), BF16)
SUMS = ((NB // 2, HD, BLK), F32)


def forward(scal, qu, kp, vp, w):
    return call(
        forward_kernel, "attention_forward",
        [(HEADS, BF16), (STATS, F32), ((4, 1, BLK), F32), (HEADS, BF16)],
        [
            ((NB * BLK, HD), BF16), ((NB, HD, BLK), BF16), (HEADS, BF16),
            (HEADS[1:], F32), (STATS[1:], F32), (STATS[1:], F32), ((1,), None),
        ],
        9 * 10**9, (11, 12, 13, 14), ALL_QUERIES, scal, qu, *kp, *vp, w,
    )


def prepare(scal, qu, kp, vp):
    return call(
        prepare_kernel, "prepare_backward",
        [(HEADS, BF16), HALF, HALF, HALF_T, HALF_T, HALF_T, HALF_T],
        [], 10**8, (), ALL_UPSTREAM, scal, qu, *kp, *vp,
    )


def upper(scal, qu, ut, qt, k, kt, vt, w, out, lse, err):
    return call(
        upper_kernel, "attention_upper",
        [((4, HPD, BLK, HD), BF16), (HEADS, BF16), (STATS, F32)]
        + [((2 * LINE + 16, BLK), BF16)] * 4,
        [SUMS, SUMS, COLUMNS, ((HPD, BLK, HD), BF16), COLUMNS, COLUMNS, (HEADS[1:], F32), ((8, BLK), F32)],
        8 * 10**9, (2, 3, 8, 9, 10, 11, 12, 13), ONE_QUERIES, scal, qu, ut, qt, k, kt, vt, w, out, lse, err,
    )


def lower(scal, qu, qt, k, kt, vt, dout, lse, delta, part):
    return call(
        lower_kernel, "attention_lower",
        [(PIECES, BF16)] + [((LINE, BLK), BF16)] * 8,
        [SUMS, SUMS, COLUMNS, ((HPD, BLK, HD), BF16), COLUMNS, COLUMNS],
        16 * 10**9, (2, 6, 7, 8, 9, 10), ONE_QUERIES, scal, qu, qt, k, kt, vt, dout, lse, delta, part,
    )


def send(x, move):
    pairs = []
    for b in range(NB):
        o, z, y = move(b // 16, b // 4 % 4, b % 4)
        pairs.append((b, 16 * o + 4 * (z % 4) + y % 4))
    return lax.ppermute(x, CTX, pairs)


def swap(x, k):
    return send(x, lambda o, z, y: (o ^ (k >> 1), z ^ (2 * (k & 1)), y))


def trade(x):
    return lax.all_to_all(x, GROUP, 0, 0, tiled=True)


def quarters(x):
    return jnp.stack([x[:, m * WIDTH:(m + 1) * WIDTH] for m in range(4)])


def from_z(x, d):
    return send(x, lambda o, z, y: (o, z - d, y))


def from_y(x, d):
    return send(x, lambda o, z, y: (o, z, y - d))


def to_z(x, d):
    return send(x, lambda o, z, y: (o, z + d, y))


def to_y(x, d):
    return send(x, lambda o, z, y: (o, z, y + d))


def halves(x):
    high = lax.reduce_precision(x, 8, 7)
    return jnp.concatenate([high, x - high], 0).astype(BF16)


def joined(x):
    return x[:8] + x[8:]


def total_of(parts):
    return functools.reduce(jnp.add, [x.astype(F32) for x in parts])


def local(queries, keys, values, segment_ids, value_weight, targets, upstream):
    o = lax.axis_index("outer")
    head = lax.axis_index("head")
    z, y = 2 * lax.axis_index("zh") + lax.axis_index("zl"), lax.axis_index("y")
    member = lax.axis_index(GROUP)

    below = jnp.sum(
        segment_ids[:, None] < jnp.arange(HD, dtype=jnp.int32)[None, :], 0, dtype=jnp.int32
    )
    below = jnp.where(jnp.arange(HD) < 8, below, 0).astype(F32).astype(BF16)
    pad = jnp.concatenate([below[None, :], jnp.zeros((PAD - 1, HD), BF16)], 0)

    def packed(index):
        k = lax.dynamic_slice_in_dim(keys, index * HD, HD, 1)
        v = lax.dynamic_slice_in_dim(values, index * HD, HD, 1)
        return jnp.concatenate([k, pad, v], 0)

    mine = packed(o)
    other = swap(packed(1 - o), 2)
    qu = trade(jnp.concatenate([quarters(queries), quarters(upstream)], 1))
    pair = jnp.stack([jnp.where(o == 0, mine, other), jnp.where(o == 0, other, mine)])
    k_pair, v_pair = pair[:, :BLK + PAD], pair[:, BLK + PAD:]
    k_line = jnp.stack([k_pair] + [from_z(k_pair, d) for d in (1, 2, 3)])
    v_line = jnp.stack([v_pair] + [from_y(v_pair, d) for d in (1, 2, 3)])
    k_line, v_line = lax.optimization_barrier((k_line, v_line))
    kp = [k_line] + [from_y(k_line, d) for d in (1, 2, 3)]
    vp = [v_line] + [from_z(v_line, d) for d in (1, 2, 3)]
    starts = jnp.sum(total_of([k[:, :, BLK, :8] for k in kp]), (0, 1)).astype(jnp.int32)
    bases = [BLK * (16 * (p >> 1) + 8 * (p & 1) + z % 2 * 4 + y) for p in range(4)]
    scal = jnp.concatenate([starts, jnp.stack(bases + [z, y, member, member]).astype(jnp.int32)])
    w = jnp.broadcast_to(
        lax.dynamic_slice_in_dim(value_weight, member * WIDTH, WIDTH, 0)[:, None], (WIDTH, HD)
    )

    out, lse, critic, qt = forward(scal, qu, kp, vp, w)

    ut, *halved = prepare(scal, qu, kp, vp)
    keys_low, keys_high = halved[0::2], halved[1::2]
    own = (jnp.arange(4)[:, None] == member) & (head == 0)
    critic = lax.psum(critic[:, 0, :] - jnp.where(own, targets[None, :], 0.0), "head")
    err = critic + sum(swap(critic, k) for k in (1, 2, 3))
    value_error = lax.dynamic_index_in_dim(err, member, 0, False)

    part, dout, delta, *grads = upper(scal, qu, ut, qt, *keys_high, w, out, lse, err[:, None, :])
    high = [grads[0]] + [to_y(grads[d], d) for d in (1, 2, 3)]
    dq, *grads = lower(scal, qu, qt, *keys_low, dout, lse, delta, part)
    high, grads = lax.optimization_barrier((high, grads))
    dk_low = [grads[0]] + [to_y(grads[d], d) for d in (1, 2, 3)]
    dv_low = [grads[4]] + [to_z(grads[4 + d], d) for d in (1, 2, 3)]
    dk_low[1], dq = lax.optimization_barrier((dk_low[1], dq))
    high = total_of(high)
    tail = halves(joined(high[2 * LINE:]))
    high = high[:2 * LINE].astype(BF16).reshape(4, 2 * HD, BLK)
    dk_low, dv_low = lax.optimization_barrier((dk_low, dv_low))
    dk_low = total_of(dk_low).astype(BF16).reshape(4, HD, BLK)
    dv_low = total_of(dv_low).astype(BF16).reshape(4, HD, BLK)
    by_z = [jnp.concatenate([dk_low[d], high[d], tail], 0) for d in range(4)]
    by_z = total_of([by_z[0]] + [to_z(by_z[d], d) for d in (1, 2, 3)])
    by_y = total_of([dv_low[0]] + [to_y(dv_low[d], d) for d in (1, 2, 3)])
    readout = joined(by_z[3 * HD:])
    low = jnp.concatenate([by_z[:HD], by_y], 0).astype(BF16)
    high = by_z[HD:3 * HD].astype(BF16)
    mine, other = jnp.where(o == 0, low, high), jnp.where(o == 0, high, low)
    other = swap(jnp.concatenate([other, halves(readout)], 0), 2)
    readout_grad = (readout + joined(other[2 * HD:].astype(F32))).reshape(-1)
    other = other[:2 * HD]
    first, second = jnp.where(o == 0, mine, other), jnp.where(o == 0, other, mine)
    key_grad = jnp.concatenate([first[:HD], second[:HD]], 0).T
    value_grad = jnp.concatenate([first[HD:], second[HD:]], 0).T

    dq = trade(dq)
    query_grad = jnp.concatenate([dq[m] for m in range(4)], 1)
    return (query_grad, key_grad, value_grad, value_error, readout_grad)


def solution(mesh):
    mesh = jax.sharding.Mesh(mesh.devices.reshape(4, 2, 2, 2, 4), ("head", *CTX))
    wide, rows_only = P(CTX, "head"), P(CTX)
    return jax.shard_map(
        local,
        mesh=mesh,
        in_specs=(wide, wide, wide, rows_only, P("head"), rows_only, wide),
        out_specs=(wide, wide, wide, rows_only, P("head")),
        check_vma=False,
    )
```

```python
import functools
import math

import jax
import jax.numpy as jnp
from jax import lax
from jax.experimental import pallas as pl
from jax.experimental.pallas import tpu as pltpu
from jax.sharding import PartitionSpec as P

HD = 128
BLK = 256
NB = 32
HPD = 4
WIDTH = HPD * HD
PAD = 16
LINE = 4 * HD
TILE = 4
SCALE = HD ** (-0.5)
SCALE2 = SCALE * math.log2(math.e)
NEG = -1e30
CTX = ("outer", "zh", "zl", "y")
GROUP = ("outer", "zh")
NT = (((1,), (1,)), ((), ()))
F32 = jnp.float32
BF16 = jnp.bfloat16
VMEM_LIMIT = 52 * 1024 * 1024


def dot(a, b):
    return jnp.dot(a, b, preferred_element_type=F32)


def dot_nt(a, b):
    return lax.dot_general(a, b, NT, preferred_element_type=F32)


def rows(b, n=1):
    return pl.ds(pl.multiple_of(b * BLK, BLK), n * BLK)


def block_of(scal, o, dz, dy):
    z = (scal[12] + dz) & 3
    y = (scal[13] + dy) & 3
    return 16 * o + 4 * z + y


def place(scal, main, rest, put_k, put_v):
    for far in range(4):
        for near in range(4):
            b = block_of(scal, 0, near, far)
            put_k(b, 0, main[far][near, :BLK, :])
            put_k(b, 1, main[far][near, BLK + PAD:2 * BLK + PAD, :])
            put_v(b, 0, main[far][near, 2 * (BLK + PAD):, :])
            put_v(block_of(scal, 0, far, near), 1, rest[far][near])


def start_of(scal, pos):
    lo = jnp.zeros_like(pos)
    for v in range(1, 8):
        lo = jnp.maximum(lo, jnp.where(pos >= scal[v], scal[v], 0))
    return lo


def allowed_of(scal, base, kb):
    query_pos = base + lax.broadcasted_iota(jnp.int32, (1, BLK), 1)
    lo = start_of(scal, query_pos)
    key_pos = kb * BLK + lax.broadcasted_iota(jnp.int32, (BLK, BLK), 0)
    return (key_pos <= query_pos) & (key_pos >= lo)


def sweep(scal, base, low, high, tile, body):
    diag = base // BLK
    first = start_of(scal, base) // BLK
    full = jnp.minimum((start_of(scal, base + BLK - 1) + BLK - 1) // BLK, diag)
    stop = jnp.clip(diag, low, high)
    full = jnp.clip(full, low, stop)
    first = jnp.clip(first, low, full)

    @pl.when((diag >= low) & (diag < high))
    def _():
        body(diag, 1, True)

    def masked(kb, c):
        body(kb, 1, True)
        return c

    def plain(t, c):
        body(full + tile * t, tile, False)
        return c

    count = (stop - full) // tile
    lax.fori_loop(first, full, masked, 0)
    lax.fori_loop(0, count, plain, 0)
    rest = full + tile * count

    @pl.when(stop - rest >= 2)
    def _():
        body(rest, 2, False)

    @pl.when((stop - rest) % 2 == 1)
    def _():
        body(stop - 1, 1, False)


def largest_norm(blocks):
    ones = jnp.ones((8, HD), BF16)
    most = jnp.zeros((8, BLK), F32)
    for x in blocks:
        most = jnp.maximum(most, dot_nt(ones, x * x))
    return jnp.max(most) * 1.02


def forward_kernel(
    scal, q_ref, k0, k1, k2, k3, v0, v1, v2, v3, w_ref,
    out_ref, lse_ref, critic_ref, qt_ref,
    k_all, vt_all, qt_all, acc, top, tot, flag,
):
    p = pl.program_id(0)

    @pl.when(p == 0)
    def _():
        norms = []
        for piece in range(4):
            for h in range(HPD):
                x = q_ref[piece, :, h * HD:(h + 1) * HD]
                qt_all[piece, h] = x.T
                norms.append(x)
        query_norm = largest_norm(norms)
        norms = []

        def put_k(b, o, blk):
            k_all[rows(b + 16 * o), :] = blk
            norms.append(blk)

        def put_v(b, o, blk):
            vt_all[b + 16 * o] = blk.T

        place(scal, (k0, k1, k2, k3), (v0, v1, v2, v3), put_k, put_v)
        small = query_norm * largest_norm(norms) * SCALE2 * SCALE2 <= 3600.0
        flag[0] = small.astype(jnp.int32)

    small = flag[0] == 1
    base = scal[8 + p]
    tot[...] = jnp.zeros_like(tot)
    acc[...] = jnp.zeros_like(acc)
    for h in range(HPD):
        qt_ref[0, h] = qt_all[p, h]

    def values_of(kb, n):
        return jnp.concatenate([vt_all[kb + t] for t in range(n)], 1)

    def bounded(kb, n, masked):
        k_blk = k_all[rows(kb, n), :]
        vt_blk = values_of(kb, n)
        if masked:
            allowed = allowed_of(scal, base, kb)
        ss = [dot(k_blk, qt_all[p, h]) for h in range(HPD)]
        probs = [jnp.exp2(s * SCALE2) for s in ss]
        if masked:
            probs = [jnp.where(allowed, x, 0.0) for x in probs]
        pv = [dot(vt_blk, x.astype(BF16)) for x in probs]
        tots = [tot[h] + jnp.sum(probs[h], 0, keepdims=True) for h in range(HPD)]
        accs = [acc[h] + pv[h] for h in range(HPD)]
        for h in range(HPD):
            tot[h] = tots[h]
            acc[h] = accs[h]

    def general(kb, n, masked):
        k_blk = k_all[rows(kb, n), :]
        vt_blk = values_of(kb, n)
        ss = [dot(k_blk, qt_all[p, h]) for h in range(HPD)]
        if masked:
            allowed = allowed_of(scal, base, kb)
            ss = [jnp.where(allowed, s, NEG) for s in ss]
        olds = [top[h] for h in range(HPD)]
        news = [jnp.maximum(olds[h], jnp.max(ss[h], 0, keepdims=True)) for h in range(HPD)]
        probs = [jnp.exp2(ss[h] * SCALE2 - news[h] * SCALE2) for h in range(HPD)]
        fades = [jnp.exp2((olds[h] - news[h]) * SCALE2) for h in range(HPD)]
        pv = [dot(vt_blk, x.astype(BF16)) for x in probs]
        tots = [tot[h] * fades[h] + jnp.sum(probs[h], 0, keepdims=True) for h in range(HPD)]
        accs = [acc[h] * fades[h] + pv[h] for h in range(HPD)]
        for h in range(HPD):
            top[h] = news[h]
            tot[h] = tots[h]
            acc[h] = accs[h]

    @pl.when(small)
    def _():
        top[...] = jnp.zeros_like(top)
        sweep(scal, base, 0, NB, TILE, bounded)

    @pl.when(jnp.logical_not(small))
    def _():
        top[...] = jnp.full_like(top, NEG)
        sweep(scal, base, 0, NB, TILE, general)

    critic = jnp.zeros((1, BLK), F32)
    for h in range(HPD):
        total = tot[h]
        out = (acc[h] / total).astype(BF16)
        out_ref[0, h] = out
        lse_ref[0, h] = top[h] * SCALE2 + jnp.log2(total)
        w = w_ref[h * HD:(h + 1) * HD, :]
        critic += jnp.sum(out.astype(F32) * jnp.concatenate([w, w], 1), 0, keepdims=True)
    critic_ref[0] = critic


def prepare_kernel(
    scal, u_ref, k0, k1, k2, k3, v0, v1, v2, v3,
    ut_ref, k_low, k_high, kt_low, kt_high, vt_low, vt_high,
):
    for p in range(4):
        for h in range(HPD):
            ut_ref[p, h] = u_ref[p, :, h * HD:(h + 1) * HD].T

    def put_k(b, o, blk):
        (k_low, k_high)[o][rows(b), :] = blk
        (kt_low, kt_high)[o][b] = blk.T

    def put_v(b, o, blk):
        (vt_low, vt_high)[o][b] = blk.T

    place(scal, (k0, k1, k2, k3), (v0, v1, v2, v3), put_k, put_v)


def spread(row):
    return jnp.broadcast_to(row, (HD, BLK)).T


def allowed_by_row(scal, base, kb):
    query_pos = base + lax.broadcasted_iota(jnp.int32, (BLK, HD), 0)
    lo = start_of(scal, query_pos)
    key_pos = kb * BLK + lax.broadcasted_iota(jnp.int32, (BLK, HD), 1)
    halves = [(x <= query_pos) & (x >= lo) for x in (key_pos, key_pos + HD)]
    return halves


def gradients(scal, low, high, q_ref, qt_ref, k_ref, kt_ref, vt_ref, do_s, dot_ref, lse_s, delta_s, dkt, dvt, dq):
    base = scal[8 + pl.program_id(0)]

    def body(kb, n, masked):
        at = kb - low
        k_blk = k_ref[rows(at, n), :]
        kt_blk = jnp.concatenate([kt_ref[at + t] for t in range(n)], 1)
        vt_blk = jnp.concatenate([vt_ref[at + t] for t in range(n)], 1)
        ss = [dot(q_ref[0, :, h * HD:(h + 1) * HD], kt_blk) for h in range(HPD)]
        dps = [dot(do_s[h], vt_blk) for h in range(HPD)]
        lses = [jnp.concatenate([lse_s[h]] * (2 * n), 1) for h in range(HPD)]
        deltas = [jnp.concatenate([delta_s[h]] * (2 * n), 1) for h in range(HPD)]
        probs = [jnp.exp2(ss[h] * SCALE2 - lses[h]) for h in range(HPD)]
        if masked:
            left, right = allowed_by_row(scal, base, kb)
            probs = [
                jnp.concatenate([jnp.where(left, x[:, :HD], 0.0), jnp.where(right, x[:, HD:], 0.0)], 1)
                for x in probs
            ]
        dls = [(probs[h] * (dps[h] - deltas[h])).astype(BF16) for h in range(HPD)]
        dv = sum(dot(dot_ref[0, h], probs[h].astype(BF16)) for h in range(HPD))
        dk = sum(dot(qt_ref[0, h], dls[h]) for h in range(HPD))
        upd = [dq[h] + dot(dls[h], k_blk) for h in range(HPD)]
        for h in range(HPD):
            dq[h] = upd[h]
        for t in range(n):
            span = slice(t * BLK, (t + 1) * BLK)
            dkt[at + t] += dk[:, span]
            dvt[at + t] += dv[:, span]

    sweep(scal, base, low, high, TILE, body)


def key_sum(dkt, b):
    return (dkt[b] * SCALE).astype(BF16)


def value_sum(dvt, b):
    return dvt[b].astype(BF16)


def upper_kernel(
    scal, q_ref, ut_ref, qt_ref, k_ref, kt_ref, vt_ref, w_ref, out_ref, lse_ref, err_ref,
    part_ref, dot_ref, delta_ref, line0, line1, line2, line3,
    dkt, dvt, dq, do_s, lse_s, delta_s, readout, readout_all,
):
    p = pl.program_id(0)

    @pl.when(p == 0)
    def _():
        dkt[...] = jnp.zeros_like(dkt)
        dvt[...] = jnp.zeros_like(dvt)
        readout[...] = jnp.zeros_like(readout)

    dq[...] = jnp.zeros_like(dq)
    err = err_ref[0]
    for h in range(HPD):
        w = w_ref[h * HD:(h + 1) * HD, :]
        w = jnp.concatenate([w, w], 1)
        out = out_ref[0, h].astype(F32)
        dout = (err * w + ut_ref[0, h].astype(F32)).astype(BF16)
        delta = jnp.sum(dout.astype(F32) * out, 0, keepdims=True)
        dot_ref[0, h] = dout
        delta_ref[0, h] = delta
        do_s[h] = dout.T
        delta_s[h] = spread(delta)
        lse_s[h] = spread(lse_ref[0, h])
        readout[h] += err * out
    gradients(
        scal, NB // 2, NB, q_ref, qt_ref, k_ref, kt_ref, vt_ref, do_s, dot_ref, lse_s, delta_s, dkt, dvt, dq
    )
    part_ref[0] = dq[...].astype(BF16)

    @pl.when(p == 3)
    def _():
        readout_all[...] = jnp.zeros_like(readout_all)
        lanes = [jnp.sum(readout[h].T, 0, keepdims=True) for h in range(HPD)]
        for r in range(2):
            readout_all[pl.ds(2 * scal[14] + r, 1), :] = jnp.concatenate(lanes[2 * r:2 * r + 2], 1)
        high = readout_all[...].astype(BF16).astype(F32)
        tail = jnp.concatenate([high, readout_all[...] - high], 0).astype(BF16)
        for dy, line in enumerate((line0, line1, line2, line3)):
            for dz in range(4):
                b = block_of(scal, 0, dz, dy)
                line[2 * dz * HD:(2 * dz + 1) * HD, :] = key_sum(dkt, b)
                line[(2 * dz + 1) * HD:(2 * dz + 2) * HD, :] = value_sum(dvt, b)
            line[2 * LINE:, :] = tail


def lower_kernel(
    scal, q_ref, qt_ref, k_ref, kt_ref, vt_ref, dot_ref, lse_ref, delta_ref, part_ref,
    dq_ref, dk0, dk1, dk2, dk3, dv0, dv1, dv2, dv3,
    dkt, dvt, dq, do_s, lse_s, delta_s,
):
    p = pl.program_id(0)

    @pl.when(p == 0)
    def _():
        dkt[...] = jnp.zeros_like(dkt)
        dvt[...] = jnp.zeros_like(dvt)

    for h in range(HPD):
        do_s[h] = dot_ref[0, h].T
        delta_s[h] = spread(delta_ref[0, h])
        lse_s[h] = spread(lse_ref[0, h])
    dq[...] = part_ref[0].astype(F32)
    gradients(
        scal, 0, NB // 2, q_ref, qt_ref, k_ref, kt_ref, vt_ref, do_s, dot_ref, lse_s, delta_s, dkt, dvt, dq
    )
    for h in range(HPD):
        dq_ref[0, :, h * HD:(h + 1) * HD] = (dq[h] * SCALE).astype(BF16)

    @pl.when(p == 3)
    def _():
        for far, (dk, dv) in enumerate(((dk0, dv0), (dk1, dv1), (dk2, dv2), (dk3, dv3))):
            for near in range(4):
                span = slice(near * HD, (near + 1) * HD)
                dk[span, :] = key_sum(dkt, block_of(scal, 0, near, far))
                dv[span, :] = value_sum(dvt, block_of(scal, 0, far, near))


SMEM_SPEC = pl.BlockSpec(memory_space=pltpu.SMEM)
VMEM_SPEC = pl.BlockSpec(memory_space=pltpu.VMEM)


def by_piece(shape):
    return pl.BlockSpec((1, *shape[1:]), lambda p: (p,) + (0,) * (len(shape) - 1))


def call(kernel, name, shapes, scratch, flops, split, part, *args):
    shapes = [jax.ShapeDtypeStruct(shape, kind) for shape, kind in shapes]
    every = [*args, *shapes]
    specs = [SMEM_SPEC] + [
        by_piece(every[t].shape) if t in split else VMEM_SPEC for t in range(1, len(every))
    ]
    if part is not None:
        specs[1] = part
    return pl.pallas_call(
        kernel,
        grid=(4 if split else 1,),
        out_shape=tuple(shapes),
        in_specs=specs[:len(args)],
        out_specs=tuple(specs[len(args):]),
        scratch_shapes=[
            pltpu.SMEM((1,), jnp.int32) if kind is None else pltpu.VMEM(shape, kind) for shape, kind in scratch
        ],
        compiler_params=pltpu.CompilerParams(vmem_limit_bytes=VMEM_LIMIT),
        cost_estimate=pl.CostEstimate(flops=flops, bytes_accessed=8 << 20, transcendentals=10**6),
        name=name,
    )(*args)


ALL_QUERIES = pl.BlockSpec((4, BLK, WIDTH), lambda p: (0, 0, 0))
ALL_UPSTREAM = pl.BlockSpec((4, BLK, WIDTH), lambda p: (0, 1, 0))
ONE_QUERIES = pl.BlockSpec((1, BLK, WIDTH), lambda p: (p, 0, 0))
HEADS = (4, HPD, HD, BLK)
STATS = (4, HPD, 1, BLK)
PIECES = (4, BLK, WIDTH)
COLUMNS = ((HPD, BLK, HD), F32)
HALF = ((NB // 2 * BLK, HD), BF16)
HALF_T = ((NB // 2, HD, BLK), BF16)
SUMS = ((NB // 2, HD, BLK), F32)


def forward(scal, qu, kp, vp, w):
    return call(
        forward_kernel, "attention_forward",
        [(HEADS, BF16), (STATS, F32), ((4, 1, BLK), F32), (HEADS, BF16)],
        [
            ((NB * BLK, HD), BF16), ((NB, HD, BLK), BF16), (HEADS, BF16),
            (HEADS[1:], F32), (STATS[1:], F32), (STATS[1:], F32), ((1,), None),
        ],
        9 * 10**9, (11, 12, 13, 14), ALL_QUERIES, scal, qu, *kp, *vp, w,
    )


def prepare(scal, qu, kp, vp):
    return call(
        prepare_kernel, "prepare_backward",
        [(HEADS, BF16), HALF, HALF, HALF_T, HALF_T, HALF_T, HALF_T],
        [], 10**8, (), ALL_UPSTREAM, scal, qu, *kp, *vp,
    )


def upper(scal, qu, ut, qt, k, kt, vt, w, out, lse, err):
    return call(
        upper_kernel, "attention_upper",
        [((4, HPD, BLK, HD), BF16), (HEADS, BF16), (STATS, F32)]
        + [((2 * LINE + 16, BLK), BF16)] * 4,
        [SUMS, SUMS, COLUMNS, ((HPD, BLK, HD), BF16), COLUMNS, COLUMNS, (HEADS[1:], F32), ((8, BLK), F32)],
        8 * 10**9, (2, 3, 8, 9, 10, 11, 12, 13), ONE_QUERIES, scal, qu, ut, qt, k, kt, vt, w, out, lse, err,
    )


def lower(scal, qu, qt, k, kt, vt, dout, lse, delta, part):
    return call(
        lower_kernel, "attention_lower",
        [(PIECES, BF16)] + [((LINE, BLK), BF16)] * 8,
        [SUMS, SUMS, COLUMNS, ((HPD, BLK, HD), BF16), COLUMNS, COLUMNS],
        16 * 10**9, (2, 6, 7, 8, 9, 10), ONE_QUERIES, scal, qu, qt, k, kt, vt, dout, lse, delta, part,
    )


def send(x, move):
    pairs = []
    for b in range(NB):
        o, z, y = move(b // 16, b // 4 % 4, b % 4)
        pairs.append((b, 16 * o + 4 * (z % 4) + y % 4))
    return lax.ppermute(x, CTX, pairs)


def swap(x, k):
    return send(x, lambda o, z, y: (o ^ (k >> 1), z ^ (2 * (k & 1)), y))


def trade(x):
    return lax.all_to_all(x, GROUP, 0, 0, tiled=True)


def quarters(x):
    return jnp.stack([x[:, m * WIDTH:(m + 1) * WIDTH] for m in range(4)])


def from_z(x, d):
    return send(x, lambda o, z, y: (o, z - d, y))


def from_y(x, d):
    return send(x, lambda o, z, y: (o, z, y - d))


def to_z(x, d):
    return send(x, lambda o, z, y: (o, z + d, y))


def to_y(x, d):
    return send(x, lambda o, z, y: (o, z, y + d))


def halves(x):
    high = lax.reduce_precision(x, 8, 7)
    return jnp.concatenate([high, x - high], 0).astype(BF16)


def joined(x):
    return x[:8] + x[8:]


def total_of(parts):
    return functools.reduce(jnp.add, [x.astype(F32) for x in parts])


def local(queries, keys, values, segment_ids, value_weight, targets, upstream):
    o = lax.axis_index("outer")
    head = lax.axis_index("head")
    z, y = 2 * lax.axis_index("zh") + lax.axis_index("zl"), lax.axis_index("y")
    member = lax.axis_index(GROUP)

    below = jnp.sum(
        segment_ids[:, None] < jnp.arange(HD, dtype=jnp.int32)[None, :], 0, dtype=jnp.int32
    )
    below = jnp.where(jnp.arange(HD) < 8, below, 0).astype(F32).astype(BF16)
    pad = jnp.concatenate([below[None, :], jnp.zeros((PAD - 1, HD), BF16)], 0)

    def packed(index):
        k = lax.dynamic_slice_in_dim(keys, index * HD, HD, 1)
        v = lax.dynamic_slice_in_dim(values, index * HD, HD, 1)
        return jnp.concatenate([k, pad, v], 0)

    mine = packed(o)
    other = swap(packed(1 - o), 2)
    low, high = jnp.where(o == 0, mine, other), jnp.where(o == 0, other, mine)
    main = jnp.concatenate([low[:BLK + PAD], high[:BLK + PAD], low[BLK + PAD:]], 0)
    rest = high[BLK + PAD:]
    main = jnp.stack([main] + [from_z(main, d) for d in (1, 2, 3)])
    rest = jnp.stack([rest] + [from_y(rest, d) for d in (1, 2, 3)])
    main, rest, queries = lax.optimization_barrier((main, rest, queries))
    kp = [main] + [from_y(main, d) for d in (1, 2, 3)]
    vp = [rest] + [from_z(rest, d) for d in (1, 2, 3)]
    qu = trade(jnp.concatenate([quarters(queries), quarters(upstream)], 1))
    counts = [k[:, r, :8] for k in kp for r in (BLK, 2 * BLK + PAD)]
    starts = jnp.sum(total_of(counts), 0).astype(jnp.int32)
    bases = [BLK * (16 * (p >> 1) + 8 * (p & 1) + z % 2 * 4 + y) for p in range(4)]
    scal = jnp.concatenate([starts, jnp.stack(bases + [z, y, member, member]).astype(jnp.int32)])
    w = jnp.broadcast_to(
        lax.dynamic_slice_in_dim(value_weight, member * WIDTH, WIDTH, 0)[:, None], (WIDTH, HD)
    )

    out, lse, critic, qt = forward(scal, qu, kp, vp, w)

    ut, *halved = prepare(scal, qu, kp, vp)
    keys_low, keys_high = halved[0::2], halved[1::2]
    own = (jnp.arange(4)[:, None] == member) & (head == 0)
    critic = lax.psum(critic[:, 0, :] - jnp.where(own, targets[None, :], 0.0), "head")
    err = critic + sum(swap(critic, k) for k in (1, 2, 3))
    value_error = lax.dynamic_index_in_dim(err, member, 0, False)

    part, dout, delta, *grads = upper(scal, qu, ut, qt, *keys_high, w, out, lse, err[:, None, :])
    high = [grads[0]] + [to_y(grads[d], d) for d in (1, 2, 3)]
    dq, *grads = lower(scal, qu, qt, *keys_low, dout, lse, delta, part)
    high, grads = lax.optimization_barrier((high, grads))
    dk_low = [grads[0]] + [to_y(grads[d], d) for d in (1, 2, 3)]
    dv_low = [grads[4]] + [to_z(grads[4 + d], d) for d in (1, 2, 3)]
    dk_low[1], dq = lax.optimization_barrier((dk_low[1], dq))
    high = total_of(high)
    tail = halves(joined(high[2 * LINE:]))
    high = high[:2 * LINE].astype(BF16).reshape(4, 2 * HD, BLK)
    dk_low, dv_low = lax.optimization_barrier((dk_low, dv_low))
    dk_low = total_of(dk_low).astype(BF16).reshape(4, HD, BLK)
    dv_low = total_of(dv_low).astype(BF16).reshape(4, HD, BLK)
    by_z = [jnp.concatenate([dk_low[d], high[d], tail], 0) for d in range(4)]
    by_z = total_of([by_z[0]] + [to_z(by_z[d], d) for d in (1, 2, 3)])
    by_y = total_of([dv_low[0]] + [to_y(dv_low[d], d) for d in (1, 2, 3)])
    readout = joined(by_z[3 * HD:])
    low = jnp.concatenate([by_z[:HD], by_y], 0).astype(BF16)
    high = by_z[HD:3 * HD].astype(BF16)
    mine, other = jnp.where(o == 0, low, high), jnp.where(o == 0, high, low)
    other = swap(jnp.concatenate([other, halves(readout)], 0), 2)
    readout_grad = (readout + joined(other[2 * HD:].astype(F32))).reshape(-1)
    other = other[:2 * HD]
    first, second = jnp.where(o == 0, mine, other), jnp.where(o == 0, other, mine)
    key_grad = jnp.concatenate([first[:HD], second[:HD]], 0).T
    value_grad = jnp.concatenate([first[HD:], second[HD:]], 0).T

    dq = trade(dq)
    query_grad = jnp.concatenate([dq[m] for m in range(4)], 1)
    return (query_grad, key_grad, value_grad, value_error, readout_grad)


def solution(mesh):
    mesh = jax.sharding.Mesh(mesh.devices.reshape(4, 2, 2, 2, 4), ("head", *CTX))
    wide, rows_only = P(CTX, "head"), P(CTX)
    return jax.shard_map(
        local,
        mesh=mesh,
        in_specs=(wide, wide, wide, rows_only, P("head"), rows_only, wide),
        out_specs=(wide, wide, wide, rows_only, P("head")),
        check_vma=False,
    )
```
